32 devices in a mesh: groups: 2 (over y), expert: 4 (over z), tensor: 4 (over x, core).
Axes of the slice: x: 2, y: 2, z: 4, core: 2. Of those that a mesh axis runs over, the one named last changes fastest.
Arguments:
- queries: bfloat16 [512, 36864], P(('groups', 'expert'), 'tensor'), parts along dimension 0, may hold values from -24 to 24
- own_latent: bfloat16 [512, 576], P(('groups', 'expert')), parts along dimension 0, may hold values from -6 to 6
- residual_in: bfloat16 [512, 3584], P(('groups', 'expert'), 'tensor'), parts along dimension 0, may hold values from -3 to 3
- row_dest: int32 [512, 1], P(('groups', 'expert')), parts along dimension 0, may hold values from 0 to 3; in each aligned block of 64 rows (0 to 63, 64 to 127, ...) at most 32 rows name the same one
- prompt_cache: bfloat16 [2048, 576], P(('groups', 'expert')), parts along dimension 0, may hold values from -6 to 6
- value_up: bfloat16 [64, 512, 128], P('tensor'), may hold values from -0.5 to 0.5
- out_proj: bfloat16 [8192, 3584], P('tensor', 'expert'), may hold values from -0.125 to 0.125
- norm_gain: bfloat16 [3584], P('tensor'), may hold values from 0.25 to 1.75
- gate_weight: bfloat16 [4, 3584, 1024], P('expert', 'tensor'), may hold values from -0.09375 to 0.09375
- up_weight: bfloat16 [4, 3584, 1024], P('expert', 'tensor'), may hold values from -0.09375 to 0.09375
- down_weight: bfloat16 [4, 1024, 3584], P('expert', None, 'tensor'), may hold values from -0.375 to 0.375
- expert_ids: int32 [512, 2], P(('groups', 'expert')), parts along dimension 0, may hold values from 0 to 3, all different within a row; in each aligned block of 64 rows (0 to 63, 64 to 127, ...) at most 48 rows name the same one
- route_weight: float32 [512, 2], P(('groups', 'expert')), parts along dimension 0, may hold values from 0.05 to 0.6
Outputs:
- scored: bfloat16 [512, 3584], P(('groups', 'expert'), 'tensor'), parts along dimension 0
The draws below stay inside these ranges and needn't reach their ends.
There are 2 independent parts, one for each index of `groups`. The reference program is written for one: setup_inputs(seed, part) draws one part's arguments, and reference() takes and returns one part's arrays. A program takes and returns all parts, laid end to end along the dimension named above; an argument that names none is the same for every part. Nothing has to cross between parts.
Inputs may be any that keep to these rules, and one draw needn't show every extreme that they name: `row_dest`: in each aligned block of 64 rows no sequence is named by more than 32 rows, and some block reaches 32. `expert_ids`: each row names 2 different experts; in each aligned block of 64 rows no expert is named by more than 48 rows, and some block reaches 48.
All inputs are finite; a program needn't handle non-finite values.
Results may differ from the reference program's by a relative error of at most 0.017.
Values may be sent and summed in bfloat16 or wider, within the bound.
No kernel may reach another device: no remote copies, remote signals or barrier semaphores. Data moves between devices by JAX's collectives and lax.ppermute only.
A program may use at most 128 MiB of HBM per device.

```python
import math
import jax
import jax.numpy as jnp
import numpy as np
from jax import lax

D = 3584
HEADS = 64
LATENT = 512
ROPE = 64
VHEAD = 128
FF = 1024
TOK_DEV = 64
PROMPT = 256
TOKENS = 256
EXPERTS = 4
TOPK = 2
CAP = 32
CAP_X = 48
N_EXPERT = 4
N_TENSOR = 4


def draw_queries(key, part):
    key = jax.random.fold_in(key, 11)
    key_width = LATENT + ROPE
    fresh_draw = jnp.clip(jax.random.normal(key, (TOKENS, HEADS, key_width), jnp.float32), -6.0, 6.0)
    return fresh_draw.reshape(TOKENS, HEADS * key_width).astype(jnp.bfloat16)


def draw_own_latent(key, part):
    key = jax.random.fold_in(key, 21)
    fresh_draw = jnp.clip(jax.random.normal(key, (TOKENS, LATENT + ROPE), jnp.float32), -6.0, 6.0)
    return fresh_draw.astype(jnp.bfloat16)


def draw_prompt_cache(key, part):
    key = jax.random.fold_in(key, 31)
    rows_all = N_EXPERT * PROMPT
    fresh_draw = jnp.clip(jax.random.normal(key, (rows_all, LATENT + ROPE), jnp.float32), -6.0, 6.0)
    return fresh_draw.astype(jnp.bfloat16)


def block_levels(own_key, shape, pieces, smallest, high):
    def one(position, blocks):
        heights = jax.random.uniform(jax.random.fold_in(jax.random.fold_in(own_key, 6), position), (blocks,), jnp.float32, smallest / len(pieces), high / len(pieces))
        return jnp.repeat(jnp.exp(heights), shape[position] // blocks).reshape((-1,) + (1,) * (len(shape) - position - 1))

    factor_of = one(*pieces[0])
    for cut in pieces[1:]:
        factor_of = factor_of * one(*cut)
    return factor_of


def shared_out(key, own, number, rows, number_of, top, most, slope):
    ranking = jax.random.permutation(key, number_of)
    heavy_load, common = shares(number_of, rows * top, most, slope, True), shares(number_of, rows * top, most, slope, False)
    places = jnp.arange(number_of)

    def named(tallies, offset_by):
        used = int((tallies > 0).sum())
        fixed = max(1, used // 4)
        shifted = fixed + (places - fixed + offset_by * (used - fixed)) % max(1, number_of - fixed)
        return jnp.zeros((number_of,), jnp.int32).at[ranking[jnp.where(places < fixed, places, shifted)]].set(jnp.asarray(tallies, jnp.int32))

    tallies = jnp.where(number % 4 == 0, named(heavy_load, number // 4), named(common, number - number // 4 - 1))
    mixed = jax.random.permutation(jax.random.fold_in(own, 3), number_of)
    giver, taker = mixed[0:number_of // 2 * 2:2], mixed[1:number_of // 2 * 2:2]
    margin = jnp.minimum(tallies[giver] - 1, most - tallies[taker]) // 2
    margin = jnp.where((giver == ranking[0]) | (taker == ranking[0]) | (tallies[taker] == 0), 0, jnp.maximum(margin, 0))
    shifted = jax.random.randint(jax.random.fold_in(own, 4), (number_of // 2,), 0, 1 << 20) % (margin + 1)
    tallies = tallies.at[giver].add(-shifted).at[taker].add(shifted)
    items = jnp.searchsorted(jnp.cumsum(tallies), jnp.arange(rows * top), side="right").astype(jnp.int32)
    table = items.reshape(top, rows).T
    table = table[jax.random.permutation(jax.random.fold_in(own, 1), rows)]
    offset_by = jax.random.randint(jax.random.fold_in(own, 2), (rows, 1), 0, top)
    return jnp.take_along_axis(table, (jnp.arange(top)[None, :] + offset_by) % top, axis=1)


def shares(amount, total, most, skew, full):
    loads = [(1 << 20) // math.isqrt(rank ** skew) + 1 for rank in range(1, amount + 1)]
    largest = most if full else min(most, max(-(-total // amount), total * loads[0] // sum(loads)))
    least = 1 if total - largest >= amount - 1 else 0
    given, spare = [largest] + [least] * (amount - 1), total - largest - least * (amount - 1)
    while spare > 0:
        free = [i for i in range(1, amount) if given[i] < largest] or [i for i in range(1, amount) if given[i] < most]
        pool, left = sum([loads[i] for i in free]), spare
        for i in free:
            extra = min(most - given[i], max(1, left * loads[i] // pool), spare)
            given[i] = given[i] + extra
            spare = spare - extra
    return np.array(given)


def gaussian(own_key, dims, deviation, bound, pieces=(), kind=jnp.bfloat16):
    drawn = jax.random.normal(own_key, dims, jnp.float32) * deviation
    if len(pieces) > 0:
        drawn = block_levels(own_key, dims, pieces, -0.22, 0.18) * drawn
    return jnp.clip(drawn, min=-bound, max=bound).astype(kind)


def setup_inputs(seed: int = 0, part: int = 0) -> dict:
    streams_of = jax.random.split(jax.random.key(seed), 14)
    part_keys = jax.random.split(jax.random.fold_in(streams_of[13], part), 14)
    queries = draw_queries(jax.random.fold_in(jax.random.fold_in(streams_of[13], part), 71), part)
    own_latent = draw_own_latent(jax.random.fold_in(jax.random.fold_in(streams_of[13], part), 71), part)
    residual_in = gaussian(part_keys[2], (TOKENS, D), 0.5, 3.0, ((0, 4), (1, 4)))
    row_dest_keys = jax.random.split(jax.random.fold_in(part_keys[3], 1), TOKENS // TOK_DEV)
    row_dest_turns = jax.random.permutation(jax.random.fold_in(part_keys[3], 3), TOKENS // TOK_DEV)
    row_dest = jax.vmap(lambda own, number: shared_out(jax.random.fold_in(part_keys[3], 2), own, number, TOK_DEV, N_EXPERT, 1, CAP, 2))(row_dest_keys, row_dest_turns).reshape((TOKENS, 1))
    prompt_cache = draw_prompt_cache(jax.random.fold_in(jax.random.fold_in(streams_of[13], part), 71), part)
    value_up = gaussian(streams_of[5], (HEADS, LATENT, VHEAD), (LATENT // 4) ** -0.5, 0.5, ((0, 4),))
    out_proj = gaussian(streams_of[6], (HEADS * VHEAD, D), (HEADS * VHEAD // 4) ** -0.5, 0.125, ((0, 4), (1, 4)))
    norm_gain = jnp.clip(1.0 + 0.15 * jax.random.normal(streams_of[7], (D,), jnp.float32), 0.25, 1.75).astype(jnp.bfloat16)
    gate_weight = gaussian(streams_of[8], (EXPERTS, D, FF), D ** -0.5, 0.09375, ((0, 4), (1, 4)))
    up_weight = gaussian(streams_of[9], (EXPERTS, D, FF), D ** -0.5, 0.09375, ((0, 4), (1, 4)))
    down_weight = gaussian(streams_of[10], (EXPERTS, FF, D), (FF // 4) ** -0.5, 0.375, ((0, 4), (2, 4)))
    expert_ids_keys = jax.random.split(jax.random.fold_in(part_keys[11], 1), TOKENS // TOK_DEV)
    expert_ids_turns = jax.random.permutation(jax.random.fold_in(part_keys[11], 3), TOKENS // TOK_DEV)
    expert_ids = jax.vmap(lambda own, number: shared_out(jax.random.fold_in(part_keys[11], 2), own, number, TOK_DEV, EXPERTS, TOPK, CAP_X, 2))(expert_ids_keys, expert_ids_turns).reshape((TOKENS, TOPK))
    route_weight = jnp.clip(jnp.exp(math.log(0.6) - 2.4849067 * jax.random.uniform(part_keys[12], (TOKENS, TOPK), jnp.float32) ** block_levels(part_keys[12], (TOKENS, TOPK), ((0, 4),), -0.2, 0.2)), 0.05, 0.6)
    return {"queries": queries, "own_latent": own_latent, "residual_in": residual_in, "row_dest": row_dest, "prompt_cache": prompt_cache, "value_up": value_up, "out_proj": out_proj, "norm_gain": norm_gain, "gate_weight": gate_weight, "up_weight": up_weight, "down_weight": down_weight, "expert_ids": expert_ids, "route_weight": route_weight}


def reference(queries, own_latent, residual_in, row_dest, prompt_cache, value_up, out_proj, norm_gain, gate_weight, up_weight, down_weight, expert_ids, route_weight):
    key_width = LATENT + ROPE
    scale = (VHEAD + ROPE) ** (-0.5)
    query_all = queries.reshape(TOKENS, HEADS, key_width)
    dest = row_dest[:, 0].astype(jnp.int32)
    value_f = value_up.astype(jnp.float32)

    def attend_row(packed):
        qrow, own, target = packed
        qrow = qrow.astype(jnp.float32)
        own = own.astype(jnp.float32)
        keys = lax.dynamic_slice_in_dim(prompt_cache, (target * PROMPT).astype(jnp.int32), PROMPT, 0).astype(jnp.float32)
        scores = jnp.einsum('hc,pc->hp', qrow, keys) * scale
        own_score = jnp.einsum('hc,c->h', qrow, own) * scale
        top = jnp.maximum(lax.optimization_barrier(jnp.max(scores, axis=1)), own_score)
        expo = jnp.exp(scores - top[:, None])
        own_e = jnp.exp(own_score - top)
        total = lax.optimization_barrier(jnp.sum(expo, axis=1)) + own_e
        probs = (expo / total[:, None]).astype(jnp.bfloat16).astype(jnp.float32)
        own_p = (own_e / total).astype(jnp.bfloat16).astype(jnp.float32)
        latent_out = jnp.einsum('hp,pl->hl', probs, keys[:, :LATENT]) + own_p[:, None] * own[None, :LATENT]
        latent_out = latent_out.astype(jnp.bfloat16).astype(jnp.float32)
        head = jnp.einsum('hl,hlv->hv', latent_out, value_f).astype(jnp.bfloat16)
        return head.reshape(HEADS * VHEAD)
    head_out = lax.map(attend_row, (query_all, own_latent, dest))
    resid = residual_in.astype(jnp.float32) + jnp.dot(head_out, out_proj, preferred_element_type=jnp.float32)
    mean_sq = lax.optimization_barrier(jnp.mean(resid * resid, axis=1))
    normed = (resid * lax.rsqrt(mean_sq + 1e-06)[:, None] * norm_gain.astype(jnp.float32)).astype(jnp.bfloat16)
    flat_ids = expert_ids.reshape(-1).astype(jnp.int32)
    assigns = TOKENS * TOPK
    most_rows = N_EXPERT * CAP_X
    order = jnp.argsort(flat_ids, stable=True).astype(jnp.int32)
    counts = lax.optimization_barrier(jnp.sum((flat_ids[:, None] == jnp.arange(EXPERTS, dtype=jnp.int32)[None, :]).astype(jnp.int32), axis=0))
    starts = (jnp.cumsum(counts) - counts).astype(jnp.int32)
    padded_order = jnp.concatenate([order, jnp.zeros((most_rows,), jnp.int32)])
    block = D // N_TENSOR

    def expert_pass(expert):
        index = lax.dynamic_slice_in_dim(padded_order, starts[expert], most_rows, 0)
        live = jnp.arange(most_rows, dtype=jnp.int32) < counts[expert]
        rows = normed[index // TOPK].astype(jnp.float32).reshape(most_rows, N_TENSOR, block)
        gate_w = gate_weight[expert].astype(jnp.float32).reshape(N_TENSOR, block, FF)
        up_w = up_weight[expert].astype(jnp.float32).reshape(N_TENSOR, block, FF)
        gate = lax.optimization_barrier(jnp.sum(jnp.einsum('rbd,bdf->rbf', rows, gate_w).astype(jnp.bfloat16).astype(jnp.float32), axis=1))
        up = lax.optimization_barrier(jnp.sum(jnp.einsum('rbd,bdf->rbf', rows, up_w).astype(jnp.bfloat16).astype(jnp.float32), axis=1))
        hidden = (jax.nn.silu(gate) * up).astype(jnp.bfloat16)
        out = jnp.dot(hidden, down_weight[expert], preferred_element_type=jnp.float32).astype(jnp.bfloat16)
        out = jnp.where(live[:, None], out.astype(jnp.float32), 0.0)
        return (index, out)
    indices, outs = lax.map(expert_pass, jnp.arange(EXPERTS, dtype=jnp.int32))
    expert_out = jnp.zeros((assigns, D), jnp.float32).at[indices.reshape(-1)].add(outs.reshape(-1, D))
    expert_out = expert_out.reshape(TOKENS, TOPK, D)
    moe = lax.optimization_barrier(jnp.sum(route_weight.astype(jnp.float32)[:, :, None] * expert_out, axis=1))
    return (resid + moe).astype(jnp.bfloat16)
```

```python
import functools

import jax
import jax.numpy as jnp
from jax import lax
from jax.experimental import pallas as pl
from jax.experimental.pallas import tpu as pltpu
from jax.sharding import PartitionSpec as P

F32 = jnp.float32
BF16 = jnp.bfloat16
VMEM = pl.BlockSpec(memory_space=pltpu.VMEM)
SMEM = pl.BlockSpec(memory_space=pltpu.SMEM)


def dot(a, b):
    return jnp.dot(a, b, preferred_element_type=F32)


def dot_t(a, b):
    return lax.dot_general(a, b, (((1,), (1,)), ((), ())), preferred_element_type=F32)


def call(kernel, outs, specs, args, flops, scratch=()):
    moved = sum(a.size * a.dtype.itemsize for a in args)
    moved += sum(o.size * o.dtype.itemsize for o in outs)
    return pl.pallas_call(
        kernel,
        out_shape=outs,
        in_specs=specs,
        out_specs=[VMEM] * len(outs),
        scratch_shapes=list(scratch),
        compiler_params=pltpu.CompilerParams(vmem_limit_bytes=32 * 1024 * 1024),
        cost_estimate=pl.CostEstimate(flops=flops, bytes_accessed=moved, transcendentals=0),
    )(*args)


def shape(dims, dtype):
    return jax.ShapeDtypeStruct(dims, dtype)


def attend_kernel(scale, group, rel_ref, q_ref, own_ref, *refs):
    keys, vup_ref, out_ref = refs[:-2], refs[-2], refs[-1]
    rows, latent = own_ref.shape[0], vup_ref.shape[1]
    heads, vhead = vup_ref.shape[0], vup_ref.shape[2]
    blocks = [keys[0][...]]
    for k in range(1, len(keys), 2):
        blocks.append(jnp.concatenate([keys[k][...], keys[k + 1][...]], axis=0))
    own = own_ref[...]
    rel = jnp.concatenate([rel_ref[...]] * group, axis=0)
    lane = lax.broadcasted_iota(jnp.int32, (rows * group, rows), 1)
    line = lax.broadcasted_iota(jnp.int32, (rows * group, rows), 0) % rows
    for first in range(0, heads, group):
        q = q_ref[first * rows : (first + group) * rows, :]
        score = dot_t(q, blocks[0])
        for k in range(1, len(blocks)):
            score = jnp.where(rel == k, dot_t(q, blocks[k]), score)
        score = score * scale
        own_score = jnp.where(lane == line, dot_t(q, own) * scale, -1e30)
        top = jnp.maximum(
            jnp.max(score, axis=1, keepdims=True), jnp.max(own_score, axis=1, keepdims=True)
        )
        expo = jnp.exp(score - top)
        own_e = jnp.exp(own_score - top)
        total = jnp.sum(expo, axis=1, keepdims=True) + jnp.sum(own_e, axis=1, keepdims=True)
        inverse = 1.0 / total
        probs = expo * inverse
        acc = dot((own_e * inverse).astype(BF16), own[:, :latent])
        for k in range(len(blocks)):
            part = jnp.where(rel == k, probs, 0.0).astype(BF16)
            acc = acc + dot(part, blocks[k][:, :latent])
        acc = acc.astype(BF16)
        for h in range(group):
            head = dot(acc[h * rows : (h + 1) * rows], vup_ref[first + h])
            out_ref[:, (first + h) * vhead : (first + h + 1) * vhead] = head.astype(BF16)


def split_store(flag, value, keep_ref, send_ref):
    half = value.shape[0] // 2

    @pl.when(flag == 0)
    def _():
        keep_ref[...] = value[:half].astype(keep_ref.dtype)
        send_ref[...] = value[half:].astype(send_ref.dtype)

    @pl.when(flag != 0)
    def _():
        keep_ref[...] = value[half:].astype(keep_ref.dtype)
        send_ref[...] = value[:half].astype(send_ref.dtype)


def project_kernel(bits_ref, h0, h1, h2, h3, w_ref, keep_ref, send_ref):
    rows = jnp.concatenate([h0[...], h1[...], h2[...], h3[...]], axis=0)
    split_store(bits_ref[0], dot(rows, w_ref[...]), keep_ref, send_ref)


def halve_kernel(bits_ref, kept_ref, got_ref, keep_ref, send_ref):
    split_store(bits_ref[1], kept_ref[...] + got_ref[...].astype(F32), keep_ref, send_ref)


def pieces(value):
    high = value.astype(BF16).astype(F32)
    middle = (value - high).astype(BF16).astype(F32)
    lane = lax.broadcasted_iota(jnp.int32, (value.shape[0], 128), 1)
    rest = jnp.where(lane == 2, value - high - middle, 0.0)
    return jnp.where(lane == 0, high, jnp.where(lane == 1, middle, rest))


def expand_kernel(bits_ref, pick_ref, a0, a1, a2, a3, gain_ref, gate_ref, up_ref, keep_ref, send_ref):
    slots = pick_ref.shape[0] // 4
    taken = [
        dot(pick_ref[k * slots : (k + 1) * slots, :], a[...]) for k, a in enumerate((a0, a1, a2, a3))
    ]
    rows = jnp.concatenate(taken, axis=0)
    squares = jnp.sum(rows * rows, axis=1, keepdims=True)
    scaled = (rows * gain_ref[...].astype(F32)).astype(BF16)
    full = jnp.concatenate(
        [dot(scaled, gate_ref[...]), dot(scaled, up_ref[...]), pieces(squares)], axis=1
    ).astype(BF16)
    split_store(bits_ref[0], full, keep_ref, send_ref)


def halve_expand_kernel(bits_ref, kept_ref, got_ref, keep_ref, send_ref):
    width = kept_ref.shape[1] - 128
    total = kept_ref[...].astype(F32) + got_ref[...].astype(F32)
    squares = jnp.sum(total[:, width:], axis=1, keepdims=True)
    total = jnp.concatenate([total[:, :width], pieces(squares)], axis=1)
    split_store(bits_ref[1], total, keep_ref, send_ref)


def hidden_kernel(features, kept_ref, got_ref, out_ref):
    ff = (kept_ref.shape[1] - 128) // 2
    total = kept_ref[...] + got_ref[...].astype(F32)
    squares = jnp.sum(total[:, 2 * ff :], axis=1, keepdims=True)
    scale = lax.rsqrt(squares / features + 1e-06)
    gate = total[:, :ff] * scale
    up = total[:, ff : 2 * ff] * scale
    out_ref[...] = (gate / (1.0 + jnp.exp(-gate)) * up).astype(BF16)


def contract_kernel(bits_ref, h0, h1, h2, h3, w_ref, o0, o1, o2, o3, held):
    slots = h0.shape[0]
    rows = jnp.concatenate([h0[...], h1[...], h2[...], h3[...]], axis=0)
    held[...] = dot(rows, w_ref[...]).astype(BF16)
    mine = 2 * bits_ref[0] + bits_ref[1]
    for k, out in enumerate((o0, o1, o2, o3)):
        start = pl.multiple_of((mine ^ k) * slots, 16)
        out[...] = held[pl.ds(start, slots), :]


def combine_kernel(put_ref, weight_ref, resid_ref, r0, r1, r2, r3, out_ref):
    total = resid_ref[...].astype(F32)
    for k, got in enumerate((r0, r1, r2, r3)):
        total = total + weight_ref[:, k : k + 1] * dot(put_ref[k], got[...])
    out_ref[...] = total.astype(BF16)


def ranks(chosen):
    count = chosen.astype(jnp.int32)
    return jnp.cumsum(count, axis=-1) - count


def square(
    queries,
    own_latent,
    residual_in,
    row_dest,
    prompt_cache,
    value_up,
    out_proj,
    norm_gain,
    gate_weight,
    up_weight,
    down_weight,
    expert_ids,
    route_weight,
):
    count = 4
    rows, width = residual_in.shape
    heads, latent, vhead = value_up.shape
    key_width = own_latent.shape[1]
    prompt = prompt_cache.shape[0]
    topk = expert_ids.shape[1]
    ff = gate_weight.shape[2]
    slots = 3 * topk * rows // (2 * count)
    scale = (vhead + key_width - latent) ** (-0.5)
    shard = lax.axis_index("expert")
    tensor = lax.axis_index("tensor")
    bits = jnp.stack([tensor % 2, tensor // 2]).astype(jnp.int32)

    def along(value, k):
        return lax.ppermute(value, "expert", [(i, (i + k) % count) for i in range(count)])

    def swap(value, mask):
        return lax.ppermute(value, "tensor", [(i, i ^ mask) for i in range(count)])

    def place(t):
        return 2 * (t % 2) + t // 2

    def target(e, t, k):
        return ((e - place(t) + k) % count) * count + e

    cells = [(e, t) for e in range(count) for t in range(count)]

    with jax.named_scope("gather_cache"):
        half = lax.dynamic_slice_in_dim(prompt_cache, (tensor % 2) * (prompt // 2), prompt // 2, 0)
        keys = [prompt_cache]
        for k in range(1, count):
            got = along(half, k)
            keys += [got, swap(got, 1)]
    with jax.named_scope("residual_to_columns"):
        resid_cols = lax.ppermute(
            residual_in, ("expert", "tensor"), [(target(e, t, 0), e * count + t) for e, t in cells]
        )
    with jax.named_scope("routing"):
        ids = [expert_ids] + [along(expert_ids, k) for k in range(1, count)]
        chosen = jnp.any(jnp.stack(ids) == shard, axis=2)
        slot = jnp.arange(slots, dtype=jnp.int32)
        pick = chosen[:, None, :] & (ranks(chosen)[:, None, :] == slot[None, :, None])
        pick = pick.astype(BF16).reshape(count * slots, rows)
        experts = (shard + jnp.arange(count, dtype=jnp.int32)) % count
        named = expert_ids[None, :, :] == experts[:, None, None]
        mine = jnp.any(named, axis=2)
        put = mine[:, :, None] & (ranks(mine)[:, :, None] == slot[None, None, :])
        put = put.astype(BF16)
        weights = jnp.sum(jnp.where(named, route_weight[None], 0.0), axis=2).T
        rel = (shard - row_dest) % count
    with jax.named_scope("query_layout"):
        q = queries.reshape(rows, heads, key_width).transpose(1, 0, 2)
        q = q.reshape(heads * rows, key_width)
    with jax.named_scope("attend"):
        group = 4
        (head_out,) = call(
            functools.partial(attend_kernel, scale, group),
            [shape((rows, heads * vhead), BF16)],
            [VMEM] * (4 + len(keys)),
            (rel, q, own_latent, *keys, value_up),
            2 * heads * rows * count * prompt * (key_width + latent),
        )
    with jax.named_scope("gather_heads"):
        gathered = [head_out] + [along(head_out, k) for k in range(1, count)]
    with jax.named_scope("project"):
        kept, sent = call(
            project_kernel,
            [shape((2 * rows, width), F32), shape((2 * rows, width), BF16)],
            [SMEM] + [VMEM] * 5,
            (bits, *gathered, out_proj),
            2 * count * rows * heads * vhead * width,
        )
        kept, sent = call(
            halve_kernel,
            [shape((rows, width), F32), shape((rows, width), BF16)],
            [SMEM, VMEM, VMEM],
            (bits, kept, swap(sent, 1)),
            2 * rows * width,
        )
        resid = (kept + swap(sent, 2).astype(F32) + resid_cols.astype(F32)).astype(BF16)
    with jax.named_scope("scatter_resid"):
        arrived = [
            lax.ppermute(
                resid, ("expert", "tensor"), [(e * count + t, target(e, t, k)) for e, t in cells]
            )
            for k in range(count)
        ]
    with jax.named_scope("expand"):
        wide = 2 * ff + 128
        kept, sent = call(
            expand_kernel,
            [shape((2 * slots, wide), BF16), shape((2 * slots, wide), BF16)],
            [SMEM] + [VMEM] * 8,
            (bits, pick, *arrived, norm_gain[None, :], gate_weight[0], up_weight[0]),
            4 * count * slots * width * ff,
        )
        kept, sent = call(
            halve_expand_kernel,
            [shape((slots, wide), F32), shape((slots, wide), BF16)],
            [SMEM, VMEM, VMEM],
            (bits, kept, swap(sent, 1)),
            2 * slots * wide,
        )
        (hidden,) = call(
            functools.partial(hidden_kernel, width * count),
            [shape((slots, ff), BF16)],
            [VMEM, VMEM],
            (kept, swap(sent, 2)),
            8 * slots * wide,
        )
    with jax.named_scope("contract"):
        across = swap(hidden, 2)
        outs = call(
            contract_kernel,
            [shape((slots, width), BF16)] * count,
            [SMEM] + [VMEM] * 5,
            (bits, hidden, across, swap(hidden, 1), swap(across, 1), down_weight[0]),
            2 * count * slots * width * ff,
            [pltpu.VMEM((count * slots, width), BF16)],
        )
    with jax.named_scope("combine"):
        back = [outs[0]] + [along(outs[k], -k) for k in range(1, count)]
        (scored,) = call(
            combine_kernel,
            [shape((rows, width), BF16)],
            [VMEM] * 7,
            (put, weights, arrived[0], *back),
            2 * count * rows * slots * width,
        )
    return scored


def slot_table(targets, count, capacity):
    onehot = (targets[:, None] == jnp.arange(count, dtype=jnp.int32)[None, :]).astype(jnp.int32)
    before = jnp.cumsum(onehot, axis=0) - onehot
    rank = jnp.sum(before * onehot, axis=1)
    return targets * capacity + rank


def general(
    queries,
    own_latent,
    residual_in,
    row_dest,
    prompt_cache,
    value_up,
    out_proj,
    norm_gain,
    gate_weight,
    up_weight,
    down_weight,
    expert_ids,
    route_weight,
):
    shards = lax.axis_size("expert")
    tok_rows = residual_in.shape[0]
    width_part = residual_in.shape[1]
    heads_here = value_up.shape[0]
    latent = value_up.shape[1]
    vhead = value_up.shape[2]
    key_width = own_latent.shape[1]
    scale = (vhead + key_width - latent) ** (-0.5)
    capacity = max(2, 2 * tok_rows // shards)
    total_slots = shards * capacity
    slot = slot_table(row_dest[:, 0], shards, capacity)
    send_query = jnp.zeros((total_slots, queries.shape[1]), queries.dtype).at[slot].set(queries)
    send_key = jnp.zeros((total_slots, key_width), own_latent.dtype).at[slot].set(own_latent)
    recv_query, recv_key = (
        lax.all_to_all(send_query, "expert", split_axis=0, concat_axis=0, tiled=True),
        lax.all_to_all(send_key, "expert", split_axis=0, concat_axis=0, tiled=True),
    )
    query_heads = recv_query.reshape(total_slots, heads_here, key_width)
    scores = (
        jnp.einsum("shc,pc->shp", query_heads, prompt_cache, preferred_element_type=jnp.float32)
        * scale
    )
    own_score = (
        jnp.einsum("shc,sc->sh", query_heads, recv_key, preferred_element_type=jnp.float32) * scale
    )
    top = jnp.maximum(jnp.max(scores, axis=2), own_score)
    expo = jnp.exp(scores - top[:, :, None])
    own_e = jnp.exp(own_score - top)
    total = jnp.sum(expo, axis=2) + own_e
    probs = (expo / total[:, :, None]).astype(jnp.bfloat16)
    own_p = (own_e / total).astype(jnp.bfloat16)
    latent_out = jnp.einsum(
        "shp,pl->shl", probs, prompt_cache[:, :latent], preferred_element_type=jnp.float32
    )
    latent_out = latent_out + own_p.astype(jnp.float32)[:, :, None] * recv_key[
        :, None, :latent
    ].astype(jnp.float32)
    latent_out = latent_out.astype(jnp.bfloat16)
    head_out = jnp.einsum(
        "shl,hlv->shv", latent_out, value_up, preferred_element_type=jnp.float32
    ).astype(jnp.bfloat16)
    head_out = head_out.reshape(total_slots, heads_here * vhead)
    returned_heads = lax.all_to_all(head_out, "expert", split_axis=0, concat_axis=0, tiled=True)
    attn_rows = returned_heads[slot]
    partial_value = jnp.dot(
        attn_rows,
        lax.all_gather(out_proj, "expert", axis=1, tiled=True),
        preferred_element_type=jnp.float32,
    )
    attn_part = lax.psum_scatter(
        partial_value.astype(jnp.bfloat16), "tensor", scatter_dimension=1, tiled=True
    ).astype(jnp.float32)
    resid = residual_in.astype(jnp.float32) + attn_part
    squares = lax.psum(jnp.sum(resid * resid, axis=1), "tensor")
    full_width = width_part * lax.axis_size("tensor")
    normed = (
        resid * lax.rsqrt(squares / full_width + 1e-06)[:, None] * norm_gain.astype(jnp.float32)
    ).astype(jnp.bfloat16)
    topk = expert_ids.shape[1]
    cap_x = 3 * topk * tok_rows // (2 * shards)
    assign_slot = slot_table(expert_ids.reshape(-1), shards, cap_x)
    assign_row = jnp.arange(tok_rows * topk, dtype=jnp.int32) // topk
    send_rows = (
        jnp.zeros((shards * cap_x, width_part), jnp.bfloat16)
        .at[assign_slot]
        .set(normed[assign_row])
    )
    arrived = lax.all_to_all(send_rows, "expert", split_axis=0, concat_axis=0, tiled=True)
    gate_part = (
        jnp.dot(arrived, gate_weight[0], preferred_element_type=jnp.float32)
        .astype(jnp.bfloat16)
        .astype(jnp.float32)
    )
    up_part = (
        jnp.dot(arrived, up_weight[0], preferred_element_type=jnp.float32)
        .astype(jnp.bfloat16)
        .astype(jnp.float32)
    )
    gate_sum, up_sum = (
        lax.psum(gate_part.astype(jnp.bfloat16), "tensor").astype(jnp.float32),
        lax.psum(up_part.astype(jnp.bfloat16), "tensor").astype(jnp.float32),
    )
    hidden = (jax.nn.silu(gate_sum) * up_sum).astype(jnp.bfloat16)
    expert_out = jnp.dot(hidden, down_weight[0], preferred_element_type=jnp.float32).astype(
        jnp.bfloat16
    )
    came_back = lax.all_to_all(expert_out, "expert", split_axis=0, concat_axis=0, tiled=True)
    picked = came_back[assign_slot].astype(jnp.float32).reshape(tok_rows, topk, width_part)
    moe = jnp.sum(route_weight[:, :, None] * picked, axis=1)
    return (resid + moe).astype(jnp.bfloat16)


def local(*args):
    if lax.axis_size("expert") == 4 and lax.axis_size("tensor") == 4:
        return square(*args)
    return general(*args)


def solution(mesh):
    return jax.shard_map(
        local,
        mesh=mesh,
        in_specs=(
            P(("groups", "expert"), "tensor"),
            P(("groups", "expert"), None),
            P(("groups", "expert"), "tensor"),
            P(("groups", "expert"), None),
            P(("groups", "expert"), None),
            P("tensor", None, None),
            P("tensor", "expert"),
            P("tensor"),
            P("expert", "tensor", None),
            P("expert", "tensor", None),
            P("expert", None, "tensor"),
            P(("groups", "expert"), None),
            P(("groups", "expert"), None),
        ),
        out_specs=P(("groups", "expert"), "tensor"),
        check_vma=False,
    )
```

```python
import functools

import jax
import jax.numpy as jnp
from jax import lax
from jax.experimental import pallas as pl
from jax.experimental.pallas import tpu as pltpu
from jax.sharding import PartitionSpec as P

F32 = jnp.float32
BF16 = jnp.bfloat16
VMEM = pl.BlockSpec(memory_space=pltpu.VMEM)
SMEM = pl.BlockSpec(memory_space=pltpu.SMEM)


def dot(a, b):
    return jnp.dot(a, b, preferred_element_type=F32)


def dot_t(a, b):
    return lax.dot_general(a, b, (((1,), (1,)), ((), ())), preferred_element_type=F32)


def call(kernel, outs, specs, args, flops, scratch=()):
    moved = sum(a.size * a.dtype.itemsize for a in args)
    moved += sum(o.size * o.dtype.itemsize for o in outs)
    return pl.pallas_call(
        kernel,
        out_shape=outs,
        in_specs=specs,
        out_specs=[VMEM] * len(outs),
        scratch_shapes=list(scratch),
        compiler_params=pltpu.CompilerParams(vmem_limit_bytes=32 * 1024 * 1024),
        cost_estimate=pl.CostEstimate(flops=flops, bytes_accessed=moved, transcendentals=0),
    )(*args)


def shape(dims, dtype):
    return jax.ShapeDtypeStruct(dims, dtype)


def attend_rows(scale, q, own, caches, wanted, rel, latent):
    rows, many = own.shape[0], q.shape[0]
    lane = lax.broadcasted_iota(jnp.int32, (many, rows), 1)
    line = lax.broadcasted_iota(jnp.int32, (many, rows), 0) % rows
    score = dot(q, caches[0])
    for cache, k in zip(caches[1:], wanted[1:]):
        score = jnp.where(rel == k, dot(q, cache), score)
    score = score * scale
    own_score = jnp.where(lane == line, dot_t(q, own) * scale, -1e30)
    top = jnp.maximum(
        jnp.max(score, axis=1, keepdims=True), jnp.max(own_score, axis=1, keepdims=True)
    )
    expo = jnp.exp(score - top)
    own_e = jnp.exp(own_score - top)
    total = jnp.sum(expo, axis=1, keepdims=True) + jnp.sum(own_e, axis=1, keepdims=True)
    inverse = 1.0 / total
    probs = expo * inverse
    acc = dot((own_e * inverse).astype(BF16), own[:, :latent])
    for cache, k in zip(caches, wanted):
        part = jnp.where(rel == k, probs, 0.0).astype(BF16)
        acc = acc + dot_t(part, cache[:latent])
    return acc


def attend_kernel(scale, group, bits_ref, rel_ref, q_ref, own_ref, *refs):
    near_ref, far, (vup_ref, out_ref, held) = refs[0], refs[1:-3], refs[-3:]
    rows = own_ref.shape[0]
    latent, vhead = vup_ref.shape[1:]
    half = far[0].shape[0]
    start = pl.multiple_of(bits_ref[0] * half, 16)
    other = pl.multiple_of((1 - bits_ref[0]) * half, 16)
    caches = [near_ref[...]]
    for k in range(len(far) // 2):
        held[k, pl.ds(start, half), :] = far[2 * k][...]
        held[k, pl.ds(other, half), :] = far[2 * k + 1][...]
        caches.append(held[k])
    rel = jnp.concatenate([rel_ref[...]] * group, axis=0)
    own = own_ref[...]
    for first in range(0, vup_ref.shape[0], group):
        q = q_ref[first * rows : (first + group) * rows, :]
        acc = attend_rows(scale, q, own, caches, range(len(caches)), rel, latent).astype(BF16)
        for h in range(group):
            head = dot(acc[h * rows : (h + 1) * rows], vup_ref[first + h])
            at = (first + h) * vhead
            out_ref[:, at : at + vhead] = head.astype(BF16)


def split_store(flag, value, keep_ref, send_ref):
    half = value.shape[0] // 2

    @pl.when(flag == 0)
    def _():
        keep_ref[...] = value[:half].astype(keep_ref.dtype)
        send_ref[...] = value[half:].astype(send_ref.dtype)

    @pl.when(flag != 0)
    def _():
        keep_ref[...] = value[half:].astype(keep_ref.dtype)
        send_ref[...] = value[:half].astype(send_ref.dtype)


def project_kernel(bits_ref, h0, h1, h2, h3, w_ref, keep_ref, send_ref, held):
    rows = h0.shape[0]
    for i, head in enumerate((h0, h1, h2, h3)):
        shard = bits_ref[2] ^ i
        position = 2 * (shard % 2) + shard // 2
        held[pl.ds(pl.multiple_of(position * rows, 16), rows), :] = head[...]
    split_store(bits_ref[0], dot(held[...], w_ref[...]), keep_ref, send_ref)


def halve_kernel(bits_ref, kept_ref, got_ref, keep_ref, send_ref):
    split_store(bits_ref[1], kept_ref[...] + got_ref[...].astype(F32), keep_ref, send_ref)


def resid_kernel(kept_ref, got_ref, given_ref, pick_ref, resid_ref, *outs):
    resid = kept_ref[...] + got_ref[...].astype(F32) + given_ref[...].astype(F32)
    resid = resid.astype(BF16)
    resid_ref[...] = resid
    for k, out in enumerate(outs):
        out[...] = dot(pick_ref[k], resid).astype(BF16)


def pieces(value):
    high = value.astype(BF16).astype(F32)
    middle = (value - high).astype(BF16).astype(F32)
    lane = lax.broadcasted_iota(jnp.int32, (value.shape[0], 128), 1)
    rest = jnp.where(lane == 2, value - high - middle, 0.0)
    return jnp.where(lane == 0, high, jnp.where(lane == 1, middle, rest))


def expand_kernel(bits_ref, a0, a1, gain_ref, gate_ref, up_ref, keep_ref, send_ref):
    rows = jnp.concatenate([a0[...], a1[...]], axis=0).astype(F32)
    squares = jnp.sum(rows * rows, axis=1, keepdims=True)
    scaled = (rows * gain_ref[...].astype(F32)).astype(BF16)
    full = jnp.concatenate(
        [dot(scaled, gate_ref[...]), dot(scaled, up_ref[...]), pieces(squares)], axis=1
    ).astype(BF16)
    split_store(bits_ref[0], full, keep_ref, send_ref)


def add_expand_kernel(kept_ref, got_ref, total_ref, send_ref):
    width = kept_ref.shape[1] - 128
    total = kept_ref[...].astype(F32) + got_ref[...].astype(F32)
    squares = jnp.sum(total[:, width:], axis=1, keepdims=True)
    total = jnp.concatenate([total[:, :width], pieces(squares)], axis=1)
    total_ref[...] = total
    send_ref[...] = total.astype(BF16)


def hidden_kernel(features, kept_ref, got_ref, out_ref):
    ff = (kept_ref.shape[1] - 128) // 2
    total = kept_ref[...] + got_ref[...].astype(F32)
    squares = jnp.sum(total[:, 2 * ff :], axis=1, keepdims=True)
    scale = lax.rsqrt(squares / features + 1e-06)
    gate = total[:, :ff] * scale
    up = total[:, ff : 2 * ff] * scale
    out_ref[...] = (gate / (1.0 + jnp.exp(-gate)) * up).astype(BF16)


def contract_kernel(bits_ref, mine_ref, other_ref, w_ref, first_ref, second_ref, held):
    slots = mine_ref.shape[0]
    held[pl.ds(pl.multiple_of(bits_ref[0] * slots, 16), slots), :] = mine_ref[...]
    held[pl.ds(pl.multiple_of((1 - bits_ref[0]) * slots, 16), slots), :] = other_ref[...]
    result = dot(held[...], w_ref[...]).astype(BF16)
    first_ref[...] = result[:slots]
    second_ref[...] = result[slots:]


def combine_kernel(put_ref, weight_ref, resid_ref, r0, r1, r2, r3, out_ref):
    total = resid_ref[...].astype(F32)
    for k, got in enumerate((r0, r1, r2, r3)):
        total = total + weight_ref[:, k : k + 1] * dot(put_ref[k], got[...])
    out_ref[...] = total.astype(BF16)


def ranks(chosen):
    count = chosen.astype(jnp.int32)
    return jnp.cumsum(count, axis=-1) - count


def square(
    queries,
    own_latent,
    residual_in,
    row_dest,
    prompt_cache,
    value_up,
    out_proj,
    norm_gain,
    gate_weight,
    up_weight,
    down_weight,
    expert_ids,
    route_weight,
):
    count = 4
    rows, width = residual_in.shape
    heads, latent, vhead = value_up.shape
    key_width = own_latent.shape[1]
    prompt = prompt_cache.shape[0]
    topk = expert_ids.shape[1]
    ff = gate_weight.shape[2]
    slots = 3 * topk * rows // (2 * count)
    scale = (vhead + key_width - latent) ** (-0.5)
    shard = lax.axis_index("expert")
    tensor = lax.axis_index("tensor")
    bits = jnp.stack([tensor % 2, tensor // 2, shard]).astype(jnp.int32)

    def across(value, mask):
        return lax.ppermute(value, "expert", [(i, i ^ mask) for i in range(count)])

    def swap(value, mask):
        return lax.ppermute(value, "tensor", [(i, i ^ mask) for i in range(count)])

    def both(value, target):
        pairs = [(e * count + t, target(e, t)) for e in range(count) for t in range(count)]
        return lax.ppermute(value, ("expert", "tensor"), pairs)

    def along(value, k):
        return lax.ppermute(value, "expert", [(i, (i + k) % count) for i in range(count)])

    def transposed(value):
        return both(value, lambda e, t: t * count + e)

    def gather(value):
        second = across(value, 2)
        return [value, across(value, 1), second, across(second, 1)]

    with jax.named_scope("gather_cache"):
        cache = prompt_cache.T
        size = key_width // 2
        half = lax.dynamic_slice_in_dim(cache, (tensor % 2) * size, size, 0)
        keys = [cache]
        for k in range(1, count):
            got = along(half, k)
            keys += [got, swap(got, 1)]
    with jax.named_scope("query_layout"):
        q = queries.reshape(rows, heads, key_width).transpose(1, 0, 2)
        q = q.reshape(heads * rows, key_width)
    with jax.named_scope("early"):
        ids, q = lax.optimization_barrier((expert_ids, q))
        ids = transposed(ids)
    with jax.named_scope("routing"):
        step = jnp.arange(count, dtype=jnp.int32)
        slot = jnp.arange(slots, dtype=jnp.int32)
        chosen = jnp.any(ids[None] == ((tensor + step) % count)[:, None, None], axis=2)
        pick = chosen[:, None, :] & (ranks(chosen)[:, None, :] == slot[None, :, None])
        pick = pick.astype(BF16)
        named = expert_ids[None] == ((shard + step) % count)[:, None, None]
        mine = jnp.any(named, axis=2)
        put = mine[:, :, None] & (ranks(mine)[:, :, None] == slot[None, None, :])
        put = put.astype(BF16)
        weights = jnp.sum(jnp.where(named, route_weight[None], 0.0), axis=2).T
        rel = (shard - row_dest) % count
    with jax.named_scope("attend"):
        group = 4
        q, pick, put, weights = lax.optimization_barrier((q, pick, put, weights))
        (head_out,) = call(
            functools.partial(attend_kernel, scale, group),
            [shape((rows, heads * vhead), BF16)],
            [SMEM] + [VMEM] * (4 + len(keys)),
            (bits, rel, q, own_latent, *keys, value_up),
            2 * heads * rows * count * prompt * (key_width + latent),
            [pltpu.VMEM((count - 1, key_width, prompt), BF16)],
        )
    with jax.named_scope("gather_heads"):
        gathered = gather(head_out)
    with jax.named_scope("project"):
        kept, sent = call(
            project_kernel,
            [shape((2 * rows, width), F32), shape((2 * rows, width), BF16)],
            [SMEM] + [VMEM] * 5,
            (bits, *gathered, out_proj),
            2 * count * rows * heads * vhead * width,
            [pltpu.VMEM((count * rows, heads * vhead), BF16)],
        )
        given, sent = lax.optimization_barrier((residual_in, sent))
        given = transposed(given)
        kept, sent = call(
            halve_kernel,
            [shape((rows, width), F32), shape((rows, width), BF16)],
            [SMEM, VMEM, VMEM],
            (bits, kept, swap(sent, 1)),
            2 * rows * width,
        )
        resid, *picked = call(
            resid_kernel,
            [shape((rows, width), BF16)] + [shape((slots, width), BF16)] * count,
            [VMEM] * 4,
            (kept, swap(sent, 2), given, pick),
            2 * count * rows * slots * width,
        )
    with jax.named_scope("scatter_resid"):
        arrived = [
            both(picked[k], lambda e, t, k=k: (t + k) % count * count + e) for k in range(count)
        ]
    wide = 2 * ff + 128
    outs = []
    for first in range(0, count, 2):
        with jax.named_scope("expand"):
            kept, sent = call(
                expand_kernel,
                [shape((slots, wide), BF16), shape((slots, wide), BF16)],
                [SMEM] + [VMEM] * 5,
                (bits, *arrived[first : first + 2], norm_gain[None, :], gate_weight[0], up_weight[0]),
                8 * slots * width * ff,
            )
            kept, sent = call(
                add_expand_kernel,
                [shape((slots, wide), F32), shape((slots, wide), BF16)],
                [VMEM, VMEM],
                (kept, swap(sent, 1)),
                2 * slots * wide,
            )
            got = swap(sent, 2)
            if first == 0:
                resid, _ = lax.optimization_barrier((resid, sent))
                resid = transposed(resid)
                resid, got = lax.optimization_barrier((resid, got))
            (hidden,) = call(
                functools.partial(hidden_kernel, width * count),
                [shape((slots, ff), BF16)],
                [VMEM, VMEM],
                (kept, got),
                8 * slots * wide,
            )
        with jax.named_scope("contract"):
            outs += call(
                contract_kernel,
                [shape((slots, width), BF16)] * 2,
                [SMEM] + [VMEM] * 3,
                (bits, hidden, swap(hidden, 1), down_weight[0]),
                4 * slots * width * ff,
                [pltpu.VMEM((2 * slots, ff), BF16)],
            )
    with jax.named_scope("combine"):
        back = [outs[0]] + [along(outs[k], -k) for k in range(1, count)]
        (scored,) = call(
            combine_kernel,
            [shape((rows, width), BF16)],
            [VMEM] * 7,
            (put, weights, resid, *back),
            2 * count * rows * slots * width,
        )
    return scored


def slot_table(targets, count, capacity):
    onehot = (targets[:, None] == jnp.arange(count, dtype=jnp.int32)[None, :]).astype(jnp.int32)
    before = jnp.cumsum(onehot, axis=0) - onehot
    rank = jnp.sum(before * onehot, axis=1)
    return targets * capacity + rank


def general(
    queries,
    own_latent,
    residual_in,
    row_dest,
    prompt_cache,
    value_up,
    out_proj,
    norm_gain,
    gate_weight,
    up_weight,
    down_weight,
    expert_ids,
    route_weight,
):
    shards = lax.axis_size("expert")
    tok_rows = residual_in.shape[0]
    width_part = residual_in.shape[1]
    heads_here = value_up.shape[0]
    latent = value_up.shape[1]
    vhead = value_up.shape[2]
    key_width = own_latent.shape[1]
    scale = (vhead + key_width - latent) ** (-0.5)
    capacity = max(2, 2 * tok_rows // shards)
    total_slots = shards * capacity
    slot = slot_table(row_dest[:, 0], shards, capacity)
    send_query = jnp.zeros((total_slots, queries.shape[1]), queries.dtype).at[slot].set(queries)
    send_key = jnp.zeros((total_slots, key_width), own_latent.dtype).at[slot].set(own_latent)
    recv_query, recv_key = (
        lax.all_to_all(send_query, "expert", split_axis=0, concat_axis=0, tiled=True),
        lax.all_to_all(send_key, "expert", split_axis=0, concat_axis=0, tiled=True),
    )
    query_heads = recv_query.reshape(total_slots, heads_here, key_width)
    scores = (
        jnp.einsum("shc,pc->shp", query_heads, prompt_cache, preferred_element_type=jnp.float32)
        * scale
    )
    own_score = (
        jnp.einsum("shc,sc->sh", query_heads, recv_key, preferred_element_type=jnp.float32) * scale
    )
    top = jnp.maximum(jnp.max(scores, axis=2), own_score)
    expo = jnp.exp(scores - top[:, :, None])
    own_e = jnp.exp(own_score - top)
    total = jnp.sum(expo, axis=2) + own_e
    probs = (expo / total[:, :, None]).astype(jnp.bfloat16)
    own_p = (own_e / total).astype(jnp.bfloat16)
    latent_out = jnp.einsum(
        "shp,pl->shl", probs, prompt_cache[:, :latent], preferred_element_type=jnp.float32
    )
    latent_out = latent_out + own_p.astype(jnp.float32)[:, :, None] * recv_key[
        :, None, :latent
    ].astype(jnp.float32)
    latent_out = latent_out.astype(jnp.bfloat16)
    head_out = jnp.einsum(
        "shl,hlv->shv", latent_out, value_up, preferred_element_type=jnp.float32
    ).astype(jnp.bfloat16)
    head_out = head_out.reshape(total_slots, heads_here * vhead)
    returned_heads = lax.all_to_all(head_out, "expert", split_axis=0, concat_axis=0, tiled=True)
    attn_rows = returned_heads[slot]
    partial_value = jnp.dot(
        attn_rows,
        lax.all_gather(out_proj, "expert", axis=1, tiled=True),
        preferred_element_type=jnp.float32,
    )
    attn_part = lax.psum_scatter(
        partial_value.astype(jnp.bfloat16), "tensor", scatter_dimension=1, tiled=True
    ).astype(jnp.float32)
    resid = residual_in.astype(jnp.float32) + attn_part
    squares = lax.psum(jnp.sum(resid * resid, axis=1), "tensor")
    full_width = width_part * lax.axis_size("tensor")
    normed = (
        resid * lax.rsqrt(squares / full_width + 1e-06)[:, None] * norm_gain.astype(jnp.float32)
    ).astype(jnp.bfloat16)
    topk = expert_ids.shape[1]
    cap_x = 3 * topk * tok_rows // (2 * shards)
    assign_slot = slot_table(expert_ids.reshape(-1), shards, cap_x)
    assign_row = jnp.arange(tok_rows * topk, dtype=jnp.int32) // topk
    send_rows = (
        jnp.zeros((shards * cap_x, width_part), jnp.bfloat16)
        .at[assign_slot]
        .set(normed[assign_row])
    )
    arrived = lax.all_to_all(send_rows, "expert", split_axis=0, concat_axis=0, tiled=True)
    gate_part = (
        jnp.dot(arrived, gate_weight[0], preferred_element_type=jnp.float32)
        .astype(jnp.bfloat16)
        .astype(jnp.float32)
    )
    up_part = (
        jnp.dot(arrived, up_weight[0], preferred_element_type=jnp.float32)
        .astype(jnp.bfloat16)
        .astype(jnp.float32)
    )
    gate_sum, up_sum = (
        lax.psum(gate_part.astype(jnp.bfloat16), "tensor").astype(jnp.float32),
        lax.psum(up_part.astype(jnp.bfloat16), "tensor").astype(jnp.float32),
    )
    hidden = (jax.nn.silu(gate_sum) * up_sum).astype(jnp.bfloat16)
    expert_out = jnp.dot(hidden, down_weight[0], preferred_element_type=jnp.float32).astype(
        jnp.bfloat16
    )
    came_back = lax.all_to_all(expert_out, "expert", split_axis=0, concat_axis=0, tiled=True)
    picked = came_back[assign_slot].astype(jnp.float32).reshape(tok_rows, topk, width_part)
    moe = jnp.sum(route_weight[:, :, None] * picked, axis=1)
    return (resid + moe).astype(jnp.bfloat16)


def local(*args):
    if lax.axis_size("expert") == 4 and lax.axis_size("tensor") == 4:
        return square(*args)
    return general(*args)


def solution(mesh):
    return jax.shard_map(
        local,
        mesh=mesh,
        in_specs=(
            P(("groups", "expert"), "tensor"),
            P(("groups", "expert"), None),
            P(("groups", "expert"), "tensor"),
            P(("groups", "expert"), None),
            P(("groups", "expert"), None),
            P("tensor", None, None),
            P("tensor", "expert"),
            P("tensor"),
            P("expert", "tensor", None),
            P("expert", "tensor", None),
            P("expert", None, "tensor"),
            P(("groups", "expert"), None),
            P(("groups", "expert"), None),
        ),
        out_specs=P(("groups", "expert"), "tensor"),
        check_vma=False,
    )
```

```python
import functools

import jax
import jax.numpy as jnp
from jax import lax
from jax.experimental import pallas as pl
from jax.experimental.pallas import tpu as pltpu
from jax.sharding import PartitionSpec as P

F32 = jnp.float32
BF16 = jnp.bfloat16
VMEM = pl.BlockSpec(memory_space=pltpu.VMEM)
SMEM = pl.BlockSpec(memory_space=pltpu.SMEM)
HBM = pl.BlockSpec(memory_space=pltpu.HBM)


def dot(a, b):
    return jnp.dot(a, b, preferred_element_type=F32)


def dot_t(a, b):
    return lax.dot_general(a, b, (((1,), (1,)), ((), ())), preferred_element_type=F32)


def call(kernel, outs, specs, args, flops, scratch=()):
    moved = sum(a.size * a.dtype.itemsize for a in args)
    moved += sum(o.size * o.dtype.itemsize for o in outs)
    return pl.pallas_call(
        kernel,
        out_shape=outs,
        in_specs=specs,
        out_specs=[VMEM] * len(outs),
        scratch_shapes=list(scratch),
        compiler_params=pltpu.CompilerParams(vmem_limit_bytes=10 * 1024 * 1024),
        cost_estimate=pl.CostEstimate(flops=flops + 1000000000, bytes_accessed=moved, transcendentals=0),
    )(*args)


def shape(dims, dtype):
    return jax.ShapeDtypeStruct(dims, dtype)


def attend_rows(scale, q, own, caches, wanted, rel, latent):
    rows, many = own.shape[0], q.shape[0]
    lane = lax.broadcasted_iota(jnp.int32, (many, rows), 1)
    line = lax.broadcasted_iota(jnp.int32, (many, rows), 0) % rows
    score = dot(q, caches[0])
    for cache, k in zip(caches[1:], wanted[1:]):
        score = jnp.where(rel == k, dot(q, cache), score)
    score = score * scale
    own_score = jnp.where(lane == line, dot_t(q, own) * scale, -1e30)
    top = jnp.maximum(
        jnp.max(score, axis=1, keepdims=True), jnp.max(own_score, axis=1, keepdims=True)
    )
    expo = jnp.exp(score - top)
    own_e = jnp.exp(own_score - top)
    total = jnp.sum(expo, axis=1, keepdims=True) + jnp.sum(own_e, axis=1, keepdims=True)
    inverse = 1.0 / total
    probs = expo * inverse
    acc = dot((own_e * inverse).astype(BF16), own[:, :latent])
    for cache, k in zip(caches, wanted):
        part = jnp.where(rel == k, probs, 0.0).astype(BF16)
        acc = acc + dot_t(part, cache[:latent])
    return acc


def collect_kernel(bits_ref, *refs):
    parts, held = refs[:-1], refs[-1]
    half = parts[0].shape[0]
    for n, part in enumerate(parts):
        start = pl.multiple_of((bits_ref[0] ^ (n & 1)) * half, 16)
        held[n // 2, pl.ds(start, half), :] = part[...]


def attend_kernel(
    scale, group, start, stop, rel_ref, q_ref, own_ref, near_ref, far_ref, vup_ref, *refs
):
    out_ref = refs[-1]
    rows = own_ref.shape[0]
    latent, vhead = vup_ref.shape[1:]
    caches = [near_ref[...]] + [far_ref[k] for k in range(far_ref.shape[0])]
    rel = jnp.concatenate([rel_ref[...]] * group, axis=0)
    own = own_ref[...]
    for first in range(start, stop, group):
        q = q_ref[first * rows : (first + group) * rows, :]
        acc = attend_rows(scale, q, own, caches, range(len(caches)), rel, latent).astype(BF16)
        for h in range(group):
            head = dot(acc[h * rows : (h + 1) * rows], vup_ref[first + h])
            at = (first + h) * vhead
            out_ref[:, at : at + vhead] = head.astype(BF16)
    if start > 0:
        out_ref[:, : start * vhead] = refs[0][...]


def split_store(flag, value, keep_ref, send_ref):
    half = value.shape[0] // 2

    @pl.when(flag == 0)
    def _():
        keep_ref[...] = value[:half].astype(keep_ref.dtype)
        send_ref[...] = value[half:].astype(send_ref.dtype)

    @pl.when(flag != 0)
    def _():
        keep_ref[...] = value[half:].astype(keep_ref.dtype)
        send_ref[...] = value[:half].astype(send_ref.dtype)


def collect_rows(bits_ref, heads, start, held):
    rows, width = held.shape[0] // len(heads), held.shape[1]
    for i, head in enumerate(heads):
        shard = bits_ref[2] ^ i
        position = 2 * (shard & 1) + (shard >> 1)
        at = start if head.shape[1] > width else 0
        held[pl.ds(pl.multiple_of(position * rows, 16), rows), :] = head[:, at : at + width]
    return held[...]


def project_first_kernel(bits_ref, h0, h1, h2, h3, w_ref, out_ref, held):
    rows = collect_rows(bits_ref, (h0, h1, h2, h3), 0, held)
    out_ref[...] = dot(rows, w_ref[: rows.shape[1], :])


def project_kernel(bits_ref, first_ref, h0, h1, h2, h3, w_ref, keep_ref, send_ref, held):
    rows = collect_rows(bits_ref, (h0, h1, h2, h3), held.shape[1], held)
    total = first_ref[...] + dot(rows, w_ref[rows.shape[1] :, :])
    split_store(bits_ref[0], total, keep_ref, send_ref)


def halve_kernel(bits_ref, kept_ref, got_ref, keep_ref, send_ref):
    split_store(bits_ref[1], kept_ref[...] + got_ref[...].astype(F32), keep_ref, send_ref)


def resid_kernel(kept_ref, got_ref, given_ref, pick_ref, resid_ref, *outs):
    resid = kept_ref[...] + got_ref[...].astype(F32) + given_ref[...].astype(F32)
    resid = resid.astype(BF16)
    resid_ref[...] = resid
    for k, out in enumerate(outs):
        out[...] = dot(pick_ref[k], resid).astype(BF16)


def pieces(value):
    high = value.astype(BF16).astype(F32)
    middle = (value - high).astype(BF16).astype(F32)
    lane = lax.broadcasted_iota(jnp.int32, (value.shape[0], 128), 1)
    rest = jnp.where(lane == 2, value - high - middle, 0.0)
    return jnp.where(lane == 0, high, jnp.where(lane == 1, middle, rest))


def expand_kernel(bits_ref, a0, a1, a2, a3, gain_ref, gate_ref, up_ref, keep_ref, send_ref):
    rows = jnp.concatenate([a0[...], a2[...], a1[...], a3[...]], axis=0).astype(F32)
    squares = jnp.sum(rows * rows, axis=1, keepdims=True)
    scaled = (rows * gain_ref[...].astype(F32)).astype(BF16)
    full = jnp.concatenate(
        [dot(scaled, gate_ref[...]), dot(scaled, up_ref[...]), pieces(squares)], axis=1
    ).astype(BF16)
    split_store(bits_ref[0], full, keep_ref, send_ref)


def add_expand_kernel(kept_ref, got_ref, *outs):
    width = kept_ref.shape[1] - 128
    total = kept_ref[...].astype(F32) + got_ref[...].astype(F32)
    squares = jnp.sum(total[:, width:], axis=1, keepdims=True)
    total = jnp.concatenate([total[:, :width], pieces(squares)], axis=1)
    slots = total.shape[0] // 2
    for n in range(2):
        part = total[n * slots : (n + 1) * slots]
        outs[2 * n][...] = part
        outs[2 * n + 1][...] = part.astype(BF16)


def hidden_kernel(features, kept_ref, got_ref, out_ref):
    ff = (kept_ref.shape[1] - 128) // 2
    total = kept_ref[...] + got_ref[...].astype(F32)
    squares = jnp.sum(total[:, 2 * ff :], axis=1, keepdims=True)
    scale = lax.rsqrt(squares / features + 1e-06)
    gate = total[:, :ff] * scale
    up = total[:, ff : 2 * ff] * scale
    out_ref[...] = (gate / (1.0 + jnp.exp(-gate)) * up).astype(BF16)


def contract_kernel(bits_ref, mine_ref, other_ref, w_ref, first_ref, second_ref, held):
    slots = mine_ref.shape[0]
    held[pl.ds(pl.multiple_of(bits_ref[0] * slots, 16), slots), :] = mine_ref[...]
    held[pl.ds(pl.multiple_of((1 - bits_ref[0]) * slots, 16), slots), :] = other_ref[...]
    result = dot(held[...], w_ref[...]).astype(BF16)
    first_ref[...] = result[:slots]
    second_ref[...] = result[slots:]


def combine_kernel(put_ref, weight_ref, resid_ref, r0, r1, r2, r3, out_ref):
    total = resid_ref[...].astype(F32)
    for k, got in enumerate((r0, r1, r2, r3)):
        total = total + weight_ref[:, k : k + 1] * dot(put_ref[k], got[...])
    out_ref[...] = total.astype(BF16)


def layout_kernel(q_ref, *refs):
    many = (len(refs) - 2) // 2
    given, out_ref, held, sems = refs[:many], refs[many], refs[many + 1 : -1], refs[-1]
    copies = [
        pltpu.make_async_copy(given[i], held[i], sems.at[i]) for i in range(many)
    ]
    for copy in copies:
        copy.start()
    rows, width = q_ref.shape[0], out_ref.shape[1]
    for h in range(q_ref.shape[1] // width):
        out_ref[h * rows : (h + 1) * rows, :] = q_ref[:, h * width : (h + 1) * width]
    for copy in copies:
        copy.wait()


def column(eye, line):
    high = line.astype(BF16).astype(F32)
    middle = (line - high).astype(BF16).astype(F32)
    parts = (high, middle, line - high - middle)
    return sum(dot_t(eye, part.astype(BF16)) for part in parts)


def chosen_slots(ids, first, count, slots, before):
    named = [ids == lax.rem(first + k, count) for k in range(count)]
    chosen = [jnp.max(n.astype(F32), axis=0, keepdims=True) for n in named]
    line = jnp.concatenate(chosen + chosen, axis=0)
    rank = dot(line.astype(BF16), before)
    slot = lax.broadcasted_iota(jnp.int32, (slots, ids.shape[1]), 0).astype(F32)
    one_hot = [
        jnp.where((slot == rank[k : k + 1]) & (chosen[k] > 0.5), 1.0, 0.0).astype(BF16)
        for k in range(count)
    ]
    return named, one_hot


def routing_kernel(
    bits_ref, ids_ref, there_ref, weight_ref, dest_ref, pick_ref, put_ref, weights_ref, rel_ref
):
    count, slots, rows = pick_ref.shape
    shard = bits_ref[2]
    tensor = bits_ref[0] + 2 * bits_ref[1]
    row = lax.broadcasted_iota(jnp.int32, (rows, rows), 0)
    lane = lax.broadcasted_iota(jnp.int32, (rows, rows), 1)
    before = jnp.where(row < lane, 1.0, 0.0).astype(BF16)
    eye = jnp.where(row == lane, 1.0, 0.0).astype(BF16)
    _, picks = chosen_slots(there_ref[...], tensor, count, slots, before)
    named, puts = chosen_slots(ids_ref[...], shard, count, slots, before)
    for k in range(count):
        pick_ref[k] = picks[k]
        put_ref[k] = dot_t(eye, puts[k]).astype(BF16)
    weight = weight_ref[...]
    lines = [jnp.sum(jnp.where(n, weight, 0.0), axis=0, keepdims=True) for n in named]
    lines.append(dest_ref[...].astype(F32))
    lines += [jnp.zeros_like(lines[0])] * (8 - len(lines))
    columns = column(eye, jnp.concatenate(lines, axis=0))
    weights_ref[...] = columns[:, :count]
    dest = columns[:, count : count + 1].astype(jnp.int32)
    rel_ref[...] = lax.rem(shard - dest + count, count)


def square(
    queries,
    own_latent,
    residual_in,
    row_dest,
    prompt_cache,
    value_up,
    out_proj,
    norm_gain,
    gate_weight,
    up_weight,
    down_weight,
    expert_ids,
    route_weight,
):
    count = 4
    rows, width = residual_in.shape
    heads, latent, vhead = value_up.shape
    key_width = own_latent.shape[1]
    prompt = prompt_cache.shape[0]
    topk = expert_ids.shape[1]
    ff = gate_weight.shape[2]
    slots = 3 * topk * rows // (2 * count)
    scale = (vhead + key_width - latent) ** (-0.5)
    shard = lax.axis_index("expert")
    tensor = lax.axis_index("tensor")
    bits = jnp.stack([tensor & 1, tensor >> 1, shard]).astype(jnp.int32)

    def across(value, mask):
        return lax.ppermute(value, "expert", [(i, i ^ mask) for i in range(count)])

    def swap(value, mask):
        return lax.ppermute(value, "tensor", [(i, i ^ mask) for i in range(count)])

    def both(value, target):
        pairs = [(e * count + t, target(e, t)) for e in range(count) for t in range(count)]
        return lax.ppermute(value, ("expert", "tensor"), pairs)

    def along(value, k):
        return lax.ppermute(value, "expert", [(i, (i + k) % count) for i in range(count)])

    def transposed(value):
        return both(value, lambda e, t: t * count + e)

    with jax.named_scope("gather_cache"):
        cache = prompt_cache.T
        size = key_width // 2
        half = lax.dynamic_slice_in_dim(cache, (tensor & 1) * size, size, 0)
        far_halves = [along(half, k) for k in range(1, count)]
    with jax.named_scope("query_layout"):
        early = (
            own_latent, cache, value_up, out_proj, gate_weight[0], up_weight[0], down_weight[0],
        )
        q, own, near, vup, proj, gate_w, up_w, down_w = pl.pallas_call(
            layout_kernel,
            out_shape=[shape((heads * rows, key_width), BF16)]
            + [pltpu.VMEM(a.shape, a.dtype) for a in early],
            in_specs=[VMEM] + [HBM] * len(early),
            out_specs=[VMEM] * (1 + len(early)),
            scratch_shapes=[pltpu.SemaphoreType.DMA((len(early),))],
            compiler_params=pltpu.CompilerParams(vmem_limit_bytes=10 * 1024 * 1024),
            cost_estimate=pl.CostEstimate(
                flops=1000000000, bytes_accessed=30000000, transcendentals=0
            ),
        )(queries, *[pltpu.with_memory_space_constraint(a, pltpu.HBM) for a in early])
    with jax.named_scope("routing"):
        there = transposed(expert_ids.T)
        pick, put, weights, rel = call(
            routing_kernel,
            [
                shape((count, slots, rows), BF16),
                shape((count, rows, slots), BF16),
                shape((rows, count), F32),
                shape((rows, 1), jnp.int32),
            ],
            [SMEM] + [VMEM] * 4,
            (bits, expert_ids.T, there, route_weight.T, row_dest.T),
            0,
        )
    with jax.named_scope("gather_cache"):
        far_halves[0], q = lax.optimization_barrier((far_halves[0], q))
        far_halves[1], pick = lax.optimization_barrier((far_halves[1], pick))
        keys = []
        for part in far_halves:
            keys += [part, swap(part, 1)]
    with jax.named_scope("attend"):
        group = 4
        (far,) = call(
            collect_kernel,
            [shape((count - 1, key_width, prompt), BF16)],
            [SMEM] + [VMEM] * len(keys),
            (bits, *keys),
            0,
        )
        given, far = lax.optimization_barrier((residual_in, far))
        given = transposed(given)
        def attend(start, stop, before):
            return call(
                functools.partial(attend_kernel, scale, group, start, stop),
                [shape((rows, stop * vhead), BF16)],
                [VMEM] * (6 + len(before)),
                (rel, q, own, near, far, vup, *before),
                2 * (stop - start) * rows * count * prompt * (key_width + latent),
            )

        (half_out,) = attend(0, heads // 2, ())
        (head_out,) = attend(heads // 2, heads, (half_out,))
    with jax.named_scope("gather_heads"):
        far_first = across(half_out, 2)
        far_second = across(head_out[:, heads // 2 * vhead :], 2)
        near_both = across(head_out, 1)
        far_first, head_out = lax.optimization_barrier((far_first, head_out))
        last_first = across(far_first, 1)
        last_second = across(far_second, 1)
        given, near_both = lax.optimization_barrier((given, near_both))
    with jax.named_scope("project"):
        (first,) = call(
            project_first_kernel,
            [shape((count * rows, width), F32)],
            [SMEM] + [VMEM] * 5,
            (bits, half_out, near_both, far_first, last_first, proj),
            count * rows * heads * vhead * width,
            [pltpu.VMEM((count * rows, heads // 2 * vhead), BF16)],
        )
        kept, sent = call(
            project_kernel,
            [shape((2 * rows, width), F32), shape((2 * rows, width), BF16)],
            [SMEM] + [VMEM] * 6,
            (bits, first, head_out, near_both, far_second, last_second, proj),
            count * rows * heads * vhead * width,
            [pltpu.VMEM((count * rows, heads // 2 * vhead), BF16)],
        )
        kept, sent = call(
            halve_kernel,
            [shape((rows, width), F32), shape((rows, width), BF16)],
            [SMEM, VMEM, VMEM],
            (bits, kept, swap(sent, 1)),
            2 * rows * width,
        )
        resid, *picked = call(
            resid_kernel,
            [shape((rows, width), BF16)] + [shape((slots, width), BF16)] * count,
            [VMEM] * 4,
            (kept, swap(sent, 2), given, pick),
            2 * count * rows * slots * width,
        )
    order = (2, 3, 0, 1)
    with jax.named_scope("scatter_resid"):
        arrived = [
            both(picked[k], lambda e, t, k=k: (t + k) % count * count + e) for k in order
        ]
    wide = 2 * ff + 128
    with jax.named_scope("expand"):
        kept, sent = call(
            expand_kernel,
            [shape((2 * slots, wide), BF16), shape((2 * slots, wide), BF16)],
            [SMEM] + [VMEM] * 7,
            (bits, *arrived, norm_gain[None, :], gate_w, up_w),
            4 * count * slots * width * ff,
        )
        halves = call(
            add_expand_kernel,
            [shape((slots, wide), F32), shape((slots, wide), BF16)] * 2,
            [VMEM, VMEM],
            (kept, swap(sent, 1)),
            2 * slots * wide,
        )
    outs = []
    for n in range(2):
        kept, sent = halves[2 * n : 2 * n + 2]
        with jax.named_scope("expand"):
            got = swap(sent, 2)
            if n == 0:
                resid, _ = lax.optimization_barrier((resid, sent))
                resid = transposed(resid)
                resid, got = lax.optimization_barrier((resid, got))
            else:
                *outs, got = lax.optimization_barrier((*outs, got))
            (hidden,) = call(
                functools.partial(hidden_kernel, width * count),
                [shape((slots, ff), BF16)],
                [VMEM, VMEM],
                (kept, got),
                8 * slots * wide,
            )
        with jax.named_scope("contract"):
            outs += call(
                contract_kernel,
                [shape((slots, width), BF16)] * 2,
                [SMEM] + [VMEM] * 3,
                (bits, hidden, swap(hidden, 1), down_w),
                4 * slots * width * ff,
                [pltpu.VMEM((2 * slots, ff), BF16)],
            )
    with jax.named_scope("combine"):
        back = [along(out, -k) if k else out for k, out in sorted(zip(order, outs), key=lambda pair: pair[0])]
        (scored,) = call(
            combine_kernel,
            [shape((rows, width), BF16)],
            [VMEM] * 7,
            (put, weights, resid, *back),
            2 * count * rows * slots * width,
        )
    return scored


def slot_table(targets, count, capacity):
    onehot = (targets[:, None] == jnp.arange(count, dtype=jnp.int32)[None, :]).astype(jnp.int32)
    before = jnp.cumsum(onehot, axis=0) - onehot
    rank = jnp.sum(before * onehot, axis=1)
    return targets * capacity + rank


def general(
    queries,
    own_latent,
    residual_in,
    row_dest,
    prompt_cache,
    value_up,
    out_proj,
    norm_gain,
    gate_weight,
    up_weight,
    down_weight,
    expert_ids,
    route_weight,
):
    shards = lax.axis_size("expert")
    tok_rows = residual_in.shape[0]
    width_part = residual_in.shape[1]
    heads_here = value_up.shape[0]
    latent = value_up.shape[1]
    vhead = value_up.shape[2]
    key_width = own_latent.shape[1]
    scale = (vhead + key_width - latent) ** (-0.5)
    capacity = max(2, 2 * tok_rows // shards)
    total_slots = shards * capacity
    slot = slot_table(row_dest[:, 0], shards, capacity)
    send_query = jnp.zeros((total_slots, queries.shape[1]), queries.dtype).at[slot].set(queries)
    send_key = jnp.zeros((total_slots, key_width), own_latent.dtype).at[slot].set(own_latent)
    recv_query, recv_key = (
        lax.all_to_all(send_query, "expert", split_axis=0, concat_axis=0, tiled=True),
        lax.all_to_all(send_key, "expert", split_axis=0, concat_axis=0, tiled=True),
    )
    query_heads = recv_query.reshape(total_slots, heads_here, key_width)
    scores = (
        jnp.einsum("shc,pc->shp", query_heads, prompt_cache, preferred_element_type=jnp.float32)
        * scale
    )
    own_score = (
        jnp.einsum("shc,sc->sh", query_heads, recv_key, preferred_element_type=jnp.float32) * scale
    )
    top = jnp.maximum(jnp.max(scores, axis=2), own_score)
    expo = jnp.exp(scores - top[:, :, None])
    own_e = jnp.exp(own_score - top)
    total = jnp.sum(expo, axis=2) + own_e
    probs = (expo / total[:, :, None]).astype(jnp.bfloat16)
    own_p = (own_e / total).astype(jnp.bfloat16)
    latent_out = jnp.einsum(
        "shp,pl->shl", probs, prompt_cache[:, :latent], preferred_element_type=jnp.float32
    )
    latent_out = latent_out + own_p.astype(jnp.float32)[:, :, None] * recv_key[
        :, None, :latent
    ].astype(jnp.float32)
    latent_out = latent_out.astype(jnp.bfloat16)
    head_out = jnp.einsum(
        "shl,hlv->shv", latent_out, value_up, preferred_element_type=jnp.float32
    ).astype(jnp.bfloat16)
    head_out = head_out.reshape(total_slots, heads_here * vhead)
    returned_heads = lax.all_to_all(head_out, "expert", split_axis=0, concat_axis=0, tiled=True)
    attn_rows = returned_heads[slot]
    partial_value = jnp.dot(
        attn_rows,
        lax.all_gather(out_proj, "expert", axis=1, tiled=True),
        preferred_element_type=jnp.float32,
    )
    attn_part = lax.psum_scatter(
        partial_value.astype(jnp.bfloat16), "tensor", scatter_dimension=1, tiled=True
    ).astype(jnp.float32)
    resid = residual_in.astype(jnp.float32) + attn_part
    squares = lax.psum(jnp.sum(resid * resid, axis=1), "tensor")
    full_width = width_part * lax.axis_size("tensor")
    normed = (
        resid * lax.rsqrt(squares / full_width + 1e-06)[:, None] * norm_gain.astype(jnp.float32)
    ).astype(jnp.bfloat16)
    topk = expert_ids.shape[1]
    cap_x = 3 * topk * tok_rows // (2 * shards)
    assign_slot = slot_table(expert_ids.reshape(-1), shards, cap_x)
    assign_row = jnp.arange(tok_rows * topk, dtype=jnp.int32) // topk
    send_rows = (
        jnp.zeros((shards * cap_x, width_part), jnp.bfloat16)
        .at[assign_slot]
        .set(normed[assign_row])
    )
    arrived = lax.all_to_all(send_rows, "expert", split_axis=0, concat_axis=0, tiled=True)
    gate_part = (
        jnp.dot(arrived, gate_weight[0], preferred_element_type=jnp.float32)
        .astype(jnp.bfloat16)
        .astype(jnp.float32)
    )
    up_part = (
        jnp.dot(arrived, up_weight[0], preferred_element_type=jnp.float32)
        .astype(jnp.bfloat16)
        .astype(jnp.float32)
    )
    gate_sum, up_sum = (
        lax.psum(gate_part.astype(jnp.bfloat16), "tensor").astype(jnp.float32),
        lax.psum(up_part.astype(jnp.bfloat16), "tensor").astype(jnp.float32),
    )
    hidden = (jax.nn.silu(gate_sum) * up_sum).astype(jnp.bfloat16)
    expert_out = jnp.dot(hidden, down_weight[0], preferred_element_type=jnp.float32).astype(
        jnp.bfloat16
    )
    came_back = lax.all_to_all(expert_out, "expert", split_axis=0, concat_axis=0, tiled=True)
    picked = came_back[assign_slot].astype(jnp.float32).reshape(tok_rows, topk, width_part)
    moe = jnp.sum(route_weight[:, :, None] * picked, axis=1)
    return (resid + moe).astype(jnp.bfloat16)


def local(*args):
    if lax.axis_size("expert") == 4 and lax.axis_size("tensor") == 4:
        return square(*args)
    return general(*args)


def solution(mesh):
    return jax.shard_map(
        local,
        mesh=mesh,
        in_specs=(
            P(("groups", "expert"), "tensor"),
            P(("groups", "expert"), None),
            P(("groups", "expert"), "tensor"),
            P(("groups", "expert"), None),
            P(("groups", "expert"), None),
            P("tensor", None, None),
            P("tensor", "expert"),
            P("tensor"),
            P("expert", "tensor", None),
            P("expert", "tensor", None),
            P("expert", None, "tensor"),
            P(("groups", "expert"), None),
            P(("groups", "expert"), None),
        ),
        out_specs=P(("groups", "expert"), "tensor"),
        check_vma=False,
    )
```

```python
import functools

import jax
import jax.numpy as jnp
from jax import lax
from jax.experimental import pallas as pl
from jax.experimental.pallas import tpu as pltpu
from jax.sharding import PartitionSpec as P

F32 = jnp.float32
BF16 = jnp.bfloat16
VMEM = pl.BlockSpec(memory_space=pltpu.VMEM)
SMEM = pl.BlockSpec(memory_space=pltpu.SMEM)
HBM = pl.BlockSpec(memory_space=pltpu.HBM)


def dot(a, b):
    return jnp.dot(a, b, preferred_element_type=F32)


def dot_t(a, b):
    return lax.dot_general(a, b, (((1,), (1,)), ((), ())), preferred_element_type=F32)


def call(kernel, outs, specs, args, flops, scratch=()):
    moved = sum(a.size * a.dtype.itemsize for a in args)
    moved += sum(o.size * o.dtype.itemsize for o in outs)
    return pl.pallas_call(
        kernel,
        out_shape=outs,
        in_specs=specs,
        out_specs=[VMEM] * len(outs),
        scratch_shapes=list(scratch),
        compiler_params=pltpu.CompilerParams(vmem_limit_bytes=10 * 1024 * 1024),
        cost_estimate=pl.CostEstimate(flops=flops + 1000000000, bytes_accessed=moved, transcendentals=0),
    )(*args)


def shape(dims, dtype):
    return jax.ShapeDtypeStruct(dims, dtype)


def attend_rows(scale, q, own, caches, wanted, rel, latent):
    rows, many = own.shape[0], q.shape[0]
    lane = lax.broadcasted_iota(jnp.int32, (many, rows), 1)
    line = lax.broadcasted_iota(jnp.int32, (many, rows), 0) % rows
    score = dot(q, caches[0])
    for cache, k in zip(caches[1:], wanted[1:]):
        score = jnp.where(rel == k, dot(q, cache), score)
    score = score * scale
    own_score = jnp.where(lane == line, dot_t(q, own) * scale, -1e30)
    top = jnp.maximum(
        jnp.max(score, axis=1, keepdims=True), jnp.max(own_score, axis=1, keepdims=True)
    )
    expo = jnp.exp(score - top)
    own_e = jnp.exp(own_score - top)
    total = jnp.sum(expo, axis=1, keepdims=True) + jnp.sum(own_e, axis=1, keepdims=True)
    inverse = 1.0 / total
    probs = expo * inverse
    acc = dot((own_e * inverse).astype(BF16), own[:, :latent])
    for cache, k in zip(caches, wanted):
        part = jnp.where(rel == k, probs, 0.0).astype(BF16)
        acc = acc + dot_t(part, cache[:latent])
    return acc


def collect_kernel(bits_ref, *refs):
    parts, held = refs[:-1], refs[-1]
    half = parts[0].shape[0]
    for n, part in enumerate(parts):
        start = pl.multiple_of((bits_ref[0] ^ (n & 1)) * half, 16)
        held[n // 2, pl.ds(start, half), :] = part[...]


def attend_kernel(
    scale, group, start, stop, rel_ref, q_ref, own_ref, near_ref, far_ref, vup_ref, out_ref
):
    rows = own_ref.shape[0]
    latent, vhead = vup_ref.shape[1:]
    caches = [near_ref[...]] + [far_ref[k] for k in range(far_ref.shape[0])]
    rel = jnp.concatenate([rel_ref[...]] * group, axis=0)
    own = own_ref[...]
    for first in range(start, stop, group):
        q = q_ref[first * rows : (first + group) * rows, :]
        acc = attend_rows(scale, q, own, caches, range(len(caches)), rel, latent).astype(BF16)
        for h in range(group):
            head = dot(acc[h * rows : (h + 1) * rows], vup_ref[first + h])
            at = (first - start + h) * vhead
            out_ref[:, at : at + vhead] = head.astype(BF16)


def split_store(flag, value, keep_ref, send_ref):
    half = value.shape[0] // 2

    @pl.when(flag == 0)
    def _():
        keep_ref[...] = value[:half].astype(keep_ref.dtype)
        send_ref[...] = value[half:].astype(send_ref.dtype)

    @pl.when(flag != 0)
    def _():
        keep_ref[...] = value[half:].astype(keep_ref.dtype)
        send_ref[...] = value[:half].astype(send_ref.dtype)


def collect_rows(bits_ref, heads, held):
    rows = heads[0].shape[0]
    for i, head in enumerate(heads):
        shard = bits_ref[2] ^ i
        position = 2 * (shard & 1) + (shard >> 1)
        held[pl.ds(pl.multiple_of(position * rows, 16), rows), :] = head[...]
    return held[...]


def project_first_kernel(bits_ref, h0, h1, h2, h3, w_ref, out_ref, held):
    rows = collect_rows(bits_ref, (h0, h1, h2, h3), held)
    out_ref[...] = dot(rows, w_ref[: rows.shape[1], :])


def project_kernel(bits_ref, first_ref, h0, h1, h2, h3, w_ref, keep_ref, send_ref, held):
    rows = collect_rows(bits_ref, (h0, h1, h2, h3), held)
    total = first_ref[...] + dot(rows, w_ref[rows.shape[1] :, :])
    split_store(bits_ref[0], total, keep_ref, send_ref)


def halve_kernel(bits_ref, kept_ref, got_ref, keep_ref, send_ref):
    split_store(bits_ref[1], kept_ref[...] + got_ref[...].astype(F32), keep_ref, send_ref)


def resid_kernel(kept_ref, got_ref, given_ref, pick_ref, resid_ref, *outs):
    resid = kept_ref[...] + got_ref[...].astype(F32) + given_ref[...].astype(F32)
    resid = resid.astype(BF16)
    resid_ref[...] = resid
    for k, out in enumerate(outs, 1):
        out[...] = dot(pick_ref[k], resid).astype(BF16)


def pieces(value):
    high = value.astype(BF16).astype(F32)
    middle = (value - high).astype(BF16).astype(F32)
    lane = lax.broadcasted_iota(jnp.int32, (value.shape[0], 128), 1)
    rest = jnp.where(lane == 2, value - high - middle, 0.0)
    return jnp.where(lane == 0, high, jnp.where(lane == 1, middle, rest))


def expand_kernel(bits_ref, pick_ref, a0, a1, own_ref, a3, gain_ref, gate_ref, up_ref, keep_ref, send_ref):
    own = dot(pick_ref[0], own_ref[...]).astype(BF16)
    rows = jnp.concatenate([a0[...], own, a1[...], a3[...]], axis=0).astype(F32)
    squares = jnp.sum(rows * rows, axis=1, keepdims=True)
    scaled = (rows * gain_ref[...].astype(F32)).astype(BF16)
    full = jnp.concatenate(
        [dot(scaled, gate_ref[...]), dot(scaled, up_ref[...]), pieces(squares)], axis=1
    ).astype(BF16)
    split_store(bits_ref[0], full, keep_ref, send_ref)


def add_expand_kernel(kept_ref, got_ref, *outs):
    width = kept_ref.shape[1] - 128
    total = kept_ref[...].astype(F32) + got_ref[...].astype(F32)
    squares = jnp.sum(total[:, width:], axis=1, keepdims=True)
    total = jnp.concatenate([total[:, :width], pieces(squares)], axis=1)
    slots = total.shape[0] // 2
    for n in range(2):
        part = total[n * slots : (n + 1) * slots]
        outs[2 * n][...] = part
        outs[2 * n + 1][...] = part.astype(BF16)


def hidden_kernel(features, kept_ref, got_ref, out_ref):
    ff = (kept_ref.shape[1] - 128) // 2
    total = kept_ref[...] + got_ref[...].astype(F32)
    squares = jnp.sum(total[:, 2 * ff :], axis=1, keepdims=True)
    scale = lax.rsqrt(squares / features + 1e-06)
    gate = total[:, :ff] * scale
    up = total[:, ff : 2 * ff] * scale
    out_ref[...] = (gate / (1.0 + jnp.exp(-gate)) * up).astype(BF16)


def contract_kernel(bits_ref, mine_ref, other_ref, w_ref, first_ref, second_ref, held):
    slots = mine_ref.shape[0]
    held[pl.ds(pl.multiple_of(bits_ref[0] * slots, 16), slots), :] = mine_ref[...]
    held[pl.ds(pl.multiple_of((1 - bits_ref[0]) * slots, 16), slots), :] = other_ref[...]
    result = dot(held[...], w_ref[...]).astype(BF16)
    first_ref[...] = result[:slots]
    second_ref[...] = result[slots:]


def combine_kernel(put_ref, weight_ref, resid_ref, r0, r1, r2, r3, out_ref):
    total = resid_ref[...].astype(F32)
    for k, got in enumerate((r0, r1, r2, r3)):
        total = total + weight_ref[:, k : k + 1] * dot(put_ref[k], got[...])
    out_ref[...] = total.astype(BF16)


def layout_kernel(q_ref, *refs):
    many = (len(refs) - 3) // 2
    given, out_ref, held, (q, sems) = refs[:many], refs[many], refs[many + 1 : -2], refs[-2:]
    copies = [pltpu.make_async_copy(q_ref, q, sems.at[many])]
    copies += [pltpu.make_async_copy(given[i], held[i], sems.at[i]) for i in range(many)]
    for copy in copies:
        copy.start()
    copies[0].wait()
    rows, width = q_ref.shape[0], out_ref.shape[1]
    for h in range(q_ref.shape[1] // width):
        out_ref[h * rows : (h + 1) * rows, :] = q[:, h * width : (h + 1) * width]
    for copy in copies[1:]:
        copy.wait()


def column(eye, line):
    high = line.astype(BF16).astype(F32)
    middle = (line - high).astype(BF16).astype(F32)
    parts = (high, middle, line - high - middle)
    return sum(dot_t(eye, part.astype(BF16)) for part in parts)


def chosen_slots(ids, first, count, slots, before):
    named = [ids == lax.rem(first + k, count) for k in range(count)]
    chosen = [jnp.max(n.astype(F32), axis=0, keepdims=True) for n in named]
    line = jnp.concatenate(chosen + chosen, axis=0)
    rank = dot(line.astype(BF16), before)
    slot = lax.broadcasted_iota(jnp.int32, (slots, ids.shape[1]), 0).astype(F32)
    one_hot = [
        jnp.where((slot == rank[k : k + 1]) & (chosen[k] > 0.5), 1.0, 0.0).astype(BF16)
        for k in range(count)
    ]
    return named, one_hot


def routing_kernel(
    bits_ref, ids_ref, there_ref, weight_ref, dest_ref, pick_ref, put_ref, weights_ref, rel_ref
):
    count, slots, rows = pick_ref.shape
    shard = bits_ref[2]
    tensor = bits_ref[0] + 2 * bits_ref[1]
    row = lax.broadcasted_iota(jnp.int32, (rows, rows), 0)
    lane = lax.broadcasted_iota(jnp.int32, (rows, rows), 1)
    before = jnp.where(row < lane, 1.0, 0.0).astype(BF16)
    eye = jnp.where(row == lane, 1.0, 0.0).astype(BF16)
    _, picks = chosen_slots(there_ref[...], tensor, count, slots, before)
    named, puts = chosen_slots(ids_ref[...], shard, count, slots, before)
    for k in range(count):
        pick_ref[k] = picks[k] if k else puts[k]
        put_ref[k] = dot_t(eye, puts[k]).astype(BF16)
    weight = weight_ref[...]
    lines = [jnp.sum(jnp.where(n, weight, 0.0), axis=0, keepdims=True) for n in named]
    lines.append(dest_ref[...].astype(F32))
    lines += [jnp.zeros_like(lines[0])] * (8 - len(lines))
    columns = column(eye, jnp.concatenate(lines, axis=0))
    weights_ref[...] = columns[:, :count]
    dest = columns[:, count : count + 1].astype(jnp.int32)
    rel_ref[...] = lax.rem(shard - dest + count, count)


def square(
    queries,
    own_latent,
    residual_in,
    row_dest,
    prompt_cache,
    value_up,
    out_proj,
    norm_gain,
    gate_weight,
    up_weight,
    down_weight,
    expert_ids,
    route_weight,
):
    count = 4
    rows, width = residual_in.shape
    heads, latent, vhead = value_up.shape
    key_width = own_latent.shape[1]
    prompt = prompt_cache.shape[0]
    topk = expert_ids.shape[1]
    ff = gate_weight.shape[2]
    slots = 3 * topk * rows // (2 * count)
    scale = (vhead + key_width - latent) ** (-0.5)
    shard = lax.axis_index("expert")
    tensor = lax.axis_index("tensor")
    bits = jnp.stack([tensor & 1, tensor >> 1, shard]).astype(jnp.int32)

    def across(value, mask):
        return lax.ppermute(value, "expert", [(i, i ^ mask) for i in range(count)])

    def swap(value, mask):
        return lax.ppermute(value, "tensor", [(i, i ^ mask) for i in range(count)])

    def both(value, target):
        pairs = [(e * count + t, target(e, t)) for e in range(count) for t in range(count)]
        return lax.ppermute(value, ("expert", "tensor"), pairs)

    def along(value, k):
        return lax.ppermute(value, "expert", [(i, (i + k) % count) for i in range(count)])

    def transposed(value):
        return both(value, lambda e, t: t * count + e)

    with jax.named_scope("gather_cache"):
        cache = prompt_cache.T
        size = key_width // 2
        half = lax.dynamic_slice_in_dim(cache, (tensor & 1) * size, size, 0)
        far_halves = [along(half, k) for k in range(1, count)]
    with jax.named_scope("query_layout"):
        early = (queries, own_latent, cache, value_up)
        q, own, near, vup = pl.pallas_call(
            layout_kernel,
            out_shape=[shape((heads * rows, key_width), BF16)]
            + [pltpu.VMEM(a.shape, a.dtype) for a in early[1:]],
            in_specs=[HBM] * len(early),
            out_specs=[VMEM] * len(early),
            scratch_shapes=[
                pltpu.VMEM(queries.shape, BF16), pltpu.SemaphoreType.DMA((len(early),))
            ],
            compiler_params=pltpu.CompilerParams(vmem_limit_bytes=10 * 1024 * 1024),
            cost_estimate=pl.CostEstimate(
                flops=1000000000, bytes_accessed=30000000, transcendentals=0
            ),
        )(*[pltpu.with_memory_space_constraint(a, pltpu.HBM) for a in early])
    with jax.named_scope("routing"):
        there = transposed(expert_ids.T)
        pick, put, weights, rel = call(
            routing_kernel,
            [
                shape((count, slots, rows), BF16),
                shape((count, rows, slots), BF16),
                shape((rows, count), F32),
                shape((rows, 1), jnp.int32),
            ],
            [SMEM] + [VMEM] * 4,
            (bits, expert_ids.T, there, route_weight.T, row_dest.T),
            0,
        )
    with jax.named_scope("gather_cache"):
        far_halves[0], q = lax.optimization_barrier((far_halves[0], q))
        far_halves[1], pick = lax.optimization_barrier((far_halves[1], pick))
        keys = []
        for part in far_halves:
            keys += [part, swap(part, 1)]
    with jax.named_scope("attend"):
        group = 4
        (far,) = call(
            collect_kernel,
            [shape((count - 1, key_width, prompt), BF16)],
            [SMEM] + [VMEM] * len(keys),
            (bits, *keys),
            0,
        )
        given, far = lax.optimization_barrier((residual_in, far))
        given = transposed(given)
        def attend(start, stop):
            return call(
                functools.partial(attend_kernel, scale, group, start, stop),
                [shape((rows, (stop - start) * vhead), BF16)],
                [VMEM] * 6,
                (rel, q, own, near, far, vup),
                2 * (stop - start) * rows * count * prompt * (key_width + latent),
            )

        (half_out,) = attend(0, heads // 2)
        (half_two,) = attend(heads // 2, heads)
    with jax.named_scope("gather_heads"):
        far_first = across(half_out, 2)
        near_first = across(half_out, 1)
        far_second = across(half_two, 2)
        far_first, near_first, half_two = lax.optimization_barrier(
            (far_first, near_first, half_two)
        )
        near_second = across(half_two, 1)
        last_first = across(far_first, 1)
        last_second = across(far_second, 1)
        given, near_second = lax.optimization_barrier((given, near_second))
    with jax.named_scope("project"):
        (first,) = call(
            project_first_kernel,
            [shape((count * rows, width), F32)],
            [SMEM] + [VMEM] * 5,
            (bits, half_out, near_first, far_first, last_first, out_proj),
            count * rows * heads * vhead * width,
            [pltpu.VMEM((count * rows, heads // 2 * vhead), BF16)],
        )
        kept, sent = call(
            project_kernel,
            [shape((2 * rows, width), F32), shape((2 * rows, width), BF16)],
            [SMEM] + [VMEM] * 6,
            (bits, first, half_two, near_second, far_second, last_second, out_proj),
            count * rows * heads * vhead * width,
            [pltpu.VMEM((count * rows, heads // 2 * vhead), BF16)],
        )
        kept, sent = call(
            halve_kernel,
            [shape((rows, width), F32), shape((rows, width), BF16)],
            [SMEM, VMEM, VMEM],
            (bits, kept, swap(sent, 1)),
            2 * rows * width,
        )
        picked = call(
            resid_kernel,
            [shape((rows, width), BF16)] + [shape((slots, width), BF16)] * (count - 1),
            [VMEM] * 4,
            (kept, swap(sent, 2), given, pick),
            2 * count * rows * slots * width,
        )
    order = (2, 3, 0, 1)
    with jax.named_scope("scatter_resid"):
        arrived = [
            both(picked[k], lambda e, t, k=k: (t + k) % count * count + e) for k in order
        ]
        resid = arrived[order.index(0)]
    wide = 2 * ff + 128
    with jax.named_scope("expand"):
        kept, sent = call(
            expand_kernel,
            [shape((2 * slots, wide), BF16), shape((2 * slots, wide), BF16)],
            [SMEM] + [VMEM] * 8,
            (bits, pick, *arrived, norm_gain[None, :], gate_weight[0], up_weight[0]),
            4 * count * slots * width * ff,
        )
        halves = call(
            add_expand_kernel,
            [shape((slots, wide), F32), shape((slots, wide), BF16)] * 2,
            [VMEM, VMEM],
            (kept, swap(sent, 1)),
            2 * slots * wide,
        )
    outs = []
    for n in range(2):
        kept, sent = halves[2 * n : 2 * n + 2]
        with jax.named_scope("expand"):
            got = swap(sent, 2)
            if n == 1:
                *outs, got = lax.optimization_barrier((*outs, got))
            (hidden,) = call(
                functools.partial(hidden_kernel, width * count),
                [shape((slots, ff), BF16)],
                [VMEM, VMEM],
                (kept, got),
                8 * slots * wide,
            )
        with jax.named_scope("contract"):
            outs += call(
                contract_kernel,
                [shape((slots, width), BF16)] * 2,
                [SMEM] + [VMEM] * 3,
                (bits, hidden, swap(hidden, 1), down_weight[0]),
                4 * slots * width * ff,
                [pltpu.VMEM((2 * slots, ff), BF16)],
            )
    with jax.named_scope("combine"):
        back = [along(out, -k) if k else out for k, out in sorted(zip(order, outs), key=lambda pair: pair[0])]
        (scored,) = call(
            combine_kernel,
            [shape((rows, width), BF16)],
            [VMEM] * 7,
            (put, weights, resid, *back),
            2 * count * rows * slots * width,
        )
    return scored


def slot_table(targets, count, capacity):
    onehot = (targets[:, None] == jnp.arange(count, dtype=jnp.int32)[None, :]).astype(jnp.int32)
    before = jnp.cumsum(onehot, axis=0) - onehot
    rank = jnp.sum(before * onehot, axis=1)
    return targets * capacity + rank


def general(
    queries,
    own_latent,
    residual_in,
    row_dest,
    prompt_cache,
    value_up,
    out_proj,
    norm_gain,
    gate_weight,
    up_weight,
    down_weight,
    expert_ids,
    route_weight,
):
    shards = lax.axis_size("expert")
    tok_rows = residual_in.shape[0]
    width_part = residual_in.shape[1]
    heads_here = value_up.shape[0]
    latent = value_up.shape[1]
    vhead = value_up.shape[2]
    key_width = own_latent.shape[1]
    scale = (vhead + key_width - latent) ** (-0.5)
    capacity = max(2, 2 * tok_rows // shards)
    total_slots = shards * capacity
    slot = slot_table(row_dest[:, 0], shards, capacity)
    send_query = jnp.zeros((total_slots, queries.shape[1]), queries.dtype).at[slot].set(queries)
    send_key = jnp.zeros((total_slots, key_width), own_latent.dtype).at[slot].set(own_latent)
    recv_query, recv_key = (
        lax.all_to_all(send_query, "expert", split_axis=0, concat_axis=0, tiled=True),
        lax.all_to_all(send_key, "expert", split_axis=0, concat_axis=0, tiled=True),
    )
    query_heads = recv_query.reshape(total_slots, heads_here, key_width)
    scores = (
        jnp.einsum("shc,pc->shp", query_heads, prompt_cache, preferred_element_type=jnp.float32)
        * scale
    )
    own_score = (
        jnp.einsum("shc,sc->sh", query_heads, recv_key, preferred_element_type=jnp.float32) * scale
    )
    top = jnp.maximum(jnp.max(scores, axis=2), own_score)
    expo = jnp.exp(scores - top[:, :, None])
    own_e = jnp.exp(own_score - top)
    total = jnp.sum(expo, axis=2) + own_e
    probs = (expo / total[:, :, None]).astype(jnp.bfloat16)
    own_p = (own_e / total).astype(jnp.bfloat16)
    latent_out = jnp.einsum(
        "shp,pl->shl", probs, prompt_cache[:, :latent], preferred_element_type=jnp.float32
    )
    latent_out = latent_out + own_p.astype(jnp.float32)[:, :, None] * recv_key[
        :, None, :latent
    ].astype(jnp.float32)
    latent_out = latent_out.astype(jnp.bfloat16)
    head_out = jnp.einsum(
        "shl,hlv->shv", latent_out, value_up, preferred_element_type=jnp.float32
    ).astype(jnp.bfloat16)
    head_out = head_out.reshape(total_slots, heads_here * vhead)
    returned_heads = lax.all_to_all(head_out, "expert", split_axis=0, concat_axis=0, tiled=True)
    attn_rows = returned_heads[slot]
    partial_value = jnp.dot(
        attn_rows,
        lax.all_gather(out_proj, "expert", axis=1, tiled=True),
        preferred_element_type=jnp.float32,
    )
    attn_part = lax.psum_scatter(
        partial_value.astype(jnp.bfloat16), "tensor", scatter_dimension=1, tiled=True
    ).astype(jnp.float32)
    resid = residual_in.astype(jnp.float32) + attn_part
    squares = lax.psum(jnp.sum(resid * resid, axis=1), "tensor")
    full_width = width_part * lax.axis_size("tensor")
    normed = (
        resid * lax.rsqrt(squares / full_width + 1e-06)[:, None] * norm_gain.astype(jnp.float32)
    ).astype(jnp.bfloat16)
    topk = expert_ids.shape[1]
    cap_x = 3 * topk * tok_rows // (2 * shards)
    assign_slot = slot_table(expert_ids.reshape(-1), shards, cap_x)
    assign_row = jnp.arange(tok_rows * topk, dtype=jnp.int32) // topk
    send_rows = (
        jnp.zeros((shards * cap_x, width_part), jnp.bfloat16)
        .at[assign_slot]
        .set(normed[assign_row])
    )
    arrived = lax.all_to_all(send_rows, "expert", split_axis=0, concat_axis=0, tiled=True)
    gate_part = (
        jnp.dot(arrived, gate_weight[0], preferred_element_type=jnp.float32)
        .astype(jnp.bfloat16)
        .astype(jnp.float32)
    )
    up_part = (
        jnp.dot(arrived, up_weight[0], preferred_element_type=jnp.float32)
        .astype(jnp.bfloat16)
        .astype(jnp.float32)
    )
    gate_sum, up_sum = (
        lax.psum(gate_part.astype(jnp.bfloat16), "tensor").astype(jnp.float32),
        lax.psum(up_part.astype(jnp.bfloat16), "tensor").astype(jnp.float32),
    )
    hidden = (jax.nn.silu(gate_sum) * up_sum).astype(jnp.bfloat16)
    expert_out = jnp.dot(hidden, down_weight[0], preferred_element_type=jnp.float32).astype(
        jnp.bfloat16
    )
    came_back = lax.all_to_all(expert_out, "expert", split_axis=0, concat_axis=0, tiled=True)
    picked = came_back[assign_slot].astype(jnp.float32).reshape(tok_rows, topk, width_part)
    moe = jnp.sum(route_weight[:, :, None] * picked, axis=1)
    return (resid + moe).astype(jnp.bfloat16)


def local(*args):
    if lax.axis_size("expert") == 4 and lax.axis_size("tensor") == 4:
        return square(*args)
    return general(*args)


def solution(mesh):
    return jax.shard_map(
        local,
        mesh=mesh,
        in_specs=(
            P(("groups", "expert"), "tensor"),
            P(("groups", "expert"), None),
            P(("groups", "expert"), "tensor"),
            P(("groups", "expert"), None),
            P(("groups", "expert"), None),
            P("tensor", None, None),
            P("tensor", "expert"),
            P("tensor"),
            P("expert", "tensor", None),
            P("expert", "tensor", None),
            P("expert", None, "tensor"),
            P(("groups", "expert"), None),
            P(("groups", "expert"), None),
        ),
        out_specs=P(("groups", "expert"), "tensor"),
        check_vma=False,
    )
```

```python
import functools

import jax
import jax.numpy as jnp
from jax import lax
from jax.experimental import pallas as pl
from jax.experimental.pallas import tpu as pltpu
from jax.sharding import PartitionSpec as P

F32 = jnp.float32
BF16 = jnp.bfloat16
VMEM = pl.BlockSpec(memory_space=pltpu.VMEM)
SMEM = pl.BlockSpec(memory_space=pltpu.SMEM)
HBM = pl.BlockSpec(memory_space=pltpu.HBM)


def dot(a, b):
    return jnp.dot(a, b, preferred_element_type=F32)


def dot_t(a, b):
    return lax.dot_general(a, b, (((1,), (1,)), ((), ())), preferred_element_type=F32)


def call(kernel, outs, specs, args, flops, scratch=()):
    moved = sum(a.size * a.dtype.itemsize for a in args)
    moved += sum(o.size * o.dtype.itemsize for o in outs)
    return pl.pallas_call(
        kernel,
        out_shape=outs,
        in_specs=specs,
        out_specs=[VMEM] * len(outs),
        scratch_shapes=list(scratch),
        compiler_params=pltpu.CompilerParams(vmem_limit_bytes=10 * 1024 * 1024),
        cost_estimate=pl.CostEstimate(flops=flops + 1000000000, bytes_accessed=moved, transcendentals=0),
    )(*args)


def shape(dims, dtype):
    return jax.ShapeDtypeStruct(dims, dtype)


def attend_rows(scale, q, own, caches, wanted, rel, latent):
    rows, many = own.shape[0], q.shape[0]
    lane = lax.broadcasted_iota(jnp.int32, (many, rows), 1)
    line = lax.broadcasted_iota(jnp.int32, (many, rows), 0) % rows
    score = dot(q, caches[0])
    for cache, k in zip(caches[1:], wanted[1:]):
        score = jnp.where(rel == k, dot(q, cache), score)
    score = score * scale
    own_score = jnp.where(lane == line, dot_t(q, own) * scale, -1e30)
    top = jnp.maximum(
        jnp.max(score, axis=1, keepdims=True), jnp.max(own_score, axis=1, keepdims=True)
    )
    expo = jnp.exp(score - top)
    own_e = jnp.exp(own_score - top)
    total = jnp.sum(expo, axis=1, keepdims=True) + jnp.sum(own_e, axis=1, keepdims=True)
    inverse = 1.0 / total
    probs = expo * inverse
    acc = dot((own_e * inverse).astype(BF16), own[:, :latent])
    for cache, k in zip(caches, wanted):
        part = jnp.where(rel == k, probs, 0.0).astype(BF16)
        acc = acc + dot_t(part, cache[:latent])
    return acc


def collect_kernel(bits_ref, *refs):
    parts, held = refs[:-1], refs[-1]
    half = parts[0].shape[0]
    for n, part in enumerate(parts):
        start = pl.multiple_of((bits_ref[0] ^ (n & 1)) * half, 16)
        held[n // 2, pl.ds(start, half), :] = part[...]


def attend_kernel(
    scale, group, start, stop, rel_ref, q_ref, own_ref, near_ref, far_ref, vup_ref, out_ref
):
    rows = own_ref.shape[0]
    latent, vhead = vup_ref.shape[1:]
    caches = [near_ref[...]] + [far_ref[k] for k in range(far_ref.shape[0])]
    rel = jnp.concatenate([rel_ref[...]] * group, axis=0)
    own = own_ref[...]
    for first in range(start, stop, group):
        q = q_ref[first * rows : (first + group) * rows, :]
        acc = attend_rows(scale, q, own, caches, range(len(caches)), rel, latent).astype(BF16)
        for h in range(group):
            head = dot(acc[h * rows : (h + 1) * rows], vup_ref[first + h])
            at = (first - start + h) * vhead
            out_ref[:, at : at + vhead] = head.astype(BF16)


def split_store(flag, value, keep_ref, send_ref):
    half = value.shape[0] // 2

    @pl.when(flag == 0)
    def _():
        keep_ref[...] = value[:half].astype(keep_ref.dtype)
        send_ref[...] = value[half:].astype(send_ref.dtype)

    @pl.when(flag != 0)
    def _():
        keep_ref[...] = value[half:].astype(keep_ref.dtype)
        send_ref[...] = value[:half].astype(send_ref.dtype)


def collect_rows(bits_ref, heads, held):
    rows = heads[0].shape[0]
    for i, head in enumerate(heads):
        shard = bits_ref[2] ^ i
        position = 2 * (shard & 1) + (shard >> 1)
        held[pl.ds(pl.multiple_of(position * rows, 16), rows), :] = head[...]
    return held[...]


def project_first_kernel(bits_ref, h0, h1, h2, h3, w_ref, out_ref, held):
    rows = collect_rows(bits_ref, (h0, h1, h2, h3), held)
    out_ref[...] = dot(rows, w_ref[: rows.shape[1], :])


def project_kernel(bits_ref, first_ref, h0, h1, h2, h3, w_ref, keep_ref, send_ref, held):
    rows = collect_rows(bits_ref, (h0, h1, h2, h3), held)
    total = first_ref[...] + dot(rows, w_ref[rows.shape[1] :, :])
    split_store(bits_ref[0], total, keep_ref, send_ref)


def halve_kernel(bits_ref, kept_ref, got_ref, keep_ref, send_ref):
    split_store(bits_ref[1], kept_ref[...] + got_ref[...].astype(F32), keep_ref, send_ref)


def resid_kernel(kept_ref, got_ref, given_ref, pick_ref, resid_ref, *outs):
    resid = kept_ref[...] + got_ref[...].astype(F32) + given_ref[...].astype(F32)
    resid = resid.astype(BF16)
    resid_ref[...] = resid
    for k, out in enumerate(outs, 1):
        out[...] = dot(pick_ref[k], resid).astype(BF16)


def pieces(value):
    high = value.astype(BF16).astype(F32)
    middle = (value - high).astype(BF16).astype(F32)
    lane = lax.broadcasted_iota(jnp.int32, (value.shape[0], 128), 1)
    rest = jnp.where(lane == 2, value - high - middle, 0.0)
    return jnp.where(lane == 0, high, jnp.where(lane == 1, middle, rest))


def expand_kernel(bits_ref, pick_ref, a0, a1, own_ref, a3, gain_ref, gate_ref, up_ref, keep_ref, send_ref):
    own = dot(pick_ref[0], own_ref[...]).astype(BF16)
    rows = jnp.concatenate([a0[...], own, a1[...], a3[...]], axis=0).astype(F32)
    squares = jnp.sum(rows * rows, axis=1, keepdims=True)
    scaled = (rows * gain_ref[...].astype(F32)).astype(BF16)
    full = jnp.concatenate(
        [dot(scaled, gate_ref[...]), dot(scaled, up_ref[...]), pieces(squares)], axis=1
    ).astype(BF16)
    split_store(bits_ref[0], full, keep_ref, send_ref)


def add_expand_kernel(kept_ref, got_ref, *outs):
    width = kept_ref.shape[1] - 128
    total = kept_ref[...].astype(F32) + got_ref[...].astype(F32)
    squares = jnp.sum(total[:, width:], axis=1, keepdims=True)
    total = jnp.concatenate([total[:, :width], pieces(squares)], axis=1)
    slots = total.shape[0] // 2
    for n in range(2):
        part = total[n * slots : (n + 1) * slots]
        outs[2 * n][...] = part
        outs[2 * n + 1][...] = part.astype(BF16)


def hidden_kernel(features, kept_ref, got_ref, out_ref):
    ff = (kept_ref.shape[1] - 128) // 2
    total = kept_ref[...] + got_ref[...].astype(F32)
    squares = jnp.sum(total[:, 2 * ff :], axis=1, keepdims=True)
    scale = lax.rsqrt(squares / features + 1e-06)
    gate = total[:, :ff] * scale
    up = total[:, ff : 2 * ff] * scale
    out_ref[...] = (gate / (1.0 + jnp.exp(-gate)) * up).astype(BF16)


def contract_kernel(bits_ref, mine_ref, other_ref, w_ref, first_ref, second_ref, held):
    slots = mine_ref.shape[0]
    held[pl.ds(pl.multiple_of(bits_ref[0] * slots, 16), slots), :] = mine_ref[...]
    held[pl.ds(pl.multiple_of((1 - bits_ref[0]) * slots, 16), slots), :] = other_ref[...]
    result = dot(held[...], w_ref[...]).astype(BF16)
    first_ref[...] = result[:slots]
    second_ref[...] = result[slots:]


def combine_early_kernel(put_ref, weight_ref, resid_ref, r0, r2, r3, out_ref):
    total = resid_ref[...].astype(F32)
    for k, got in ((0, r0), (2, r2), (3, r3)):
        total = total + weight_ref[:, k : k + 1] * dot(put_ref[k], got[...])
    out_ref[...] = total


def combine_kernel(put_ref, weight_ref, early_ref, r1, out_ref):
    total = early_ref[...] + weight_ref[:, 1:2] * dot(put_ref[1], r1[...])
    out_ref[...] = total.astype(BF16)


def layout_kernel(q_ref, *refs):
    many = (len(refs) - 3) // 2
    given, out_ref, held, (q, sems) = refs[:many], refs[many], refs[many + 1 : -2], refs[-2:]
    copies = [pltpu.make_async_copy(q_ref, q, sems.at[many])]
    copies += [pltpu.make_async_copy(given[i], held[i], sems.at[i]) for i in range(many)]
    for copy in copies:
        copy.start()
    copies[0].wait()
    rows, width = q_ref.shape[0], out_ref.shape[1]
    for h in range(q_ref.shape[1] // width):
        out_ref[h * rows : (h + 1) * rows, :] = q[:, h * width : (h + 1) * width]
    for copy in copies[1:]:
        copy.wait()


def column(eye, line):
    high = line.astype(BF16).astype(F32)
    middle = (line - high).astype(BF16).astype(F32)
    parts = (high, middle, line - high - middle)
    return sum(dot_t(eye, part.astype(BF16)) for part in parts)


def chosen_slots(ids, first, count, slots, before):
    named = [ids == lax.rem(first + k, count) for k in range(count)]
    chosen = [jnp.max(n.astype(F32), axis=0, keepdims=True) for n in named]
    line = jnp.concatenate(chosen + chosen, axis=0)
    rank = dot(line.astype(BF16), before)
    slot = lax.broadcasted_iota(jnp.int32, (slots, ids.shape[1]), 0).astype(F32)
    one_hot = [
        jnp.where((slot == rank[k : k + 1]) & (chosen[k] > 0.5), 1.0, 0.0).astype(BF16)
        for k in range(count)
    ]
    return named, one_hot


def routing_kernel(
    bits_ref, ids_ref, there_ref, weight_ref, dest_ref, pick_ref, put_ref, weights_ref, rel_ref
):
    count, slots, rows = pick_ref.shape
    shard = bits_ref[2]
    tensor = bits_ref[0] + 2 * bits_ref[1]
    row = lax.broadcasted_iota(jnp.int32, (rows, rows), 0)
    lane = lax.broadcasted_iota(jnp.int32, (rows, rows), 1)
    before = jnp.where(row < lane, 1.0, 0.0).astype(BF16)
    eye = jnp.where(row == lane, 1.0, 0.0).astype(BF16)
    _, picks = chosen_slots(there_ref[...], tensor, count, slots, before)
    named, puts = chosen_slots(ids_ref[...], shard, count, slots, before)
    for k in range(count):
        pick_ref[k] = picks[k] if k else puts[k]
        put_ref[k] = dot_t(eye, puts[k]).astype(BF16)
    weight = weight_ref[...]
    lines = [jnp.sum(jnp.where(n, weight, 0.0), axis=0, keepdims=True) for n in named]
    lines.append(dest_ref[...].astype(F32))
    lines += [jnp.zeros_like(lines[0])] * (8 - len(lines))
    columns = column(eye, jnp.concatenate(lines, axis=0))
    weights_ref[...] = columns[:, :count]
    dest = columns[:, count : count + 1].astype(jnp.int32)
    rel_ref[...] = lax.rem(shard - dest + count, count)


def square(
    queries,
    own_latent,
    residual_in,
    row_dest,
    prompt_cache,
    value_up,
    out_proj,
    norm_gain,
    gate_weight,
    up_weight,
    down_weight,
    expert_ids,
    route_weight,
):
    count = 4
    rows, width = residual_in.shape
    heads, latent, vhead = value_up.shape
    key_width = own_latent.shape[1]
    prompt = prompt_cache.shape[0]
    topk = expert_ids.shape[1]
    ff = gate_weight.shape[2]
    slots = 3 * topk * rows // (2 * count)
    scale = (vhead + key_width - latent) ** (-0.5)
    shard = lax.axis_index("expert")
    tensor = lax.axis_index("tensor")
    bits = jnp.stack([tensor & 1, tensor >> 1, shard]).astype(jnp.int32)

    def across(value, mask):
        return lax.ppermute(value, "expert", [(i, i ^ mask) for i in range(count)])

    def swap(value, mask):
        return lax.ppermute(value, "tensor", [(i, i ^ mask) for i in range(count)])

    def both(value, target):
        pairs = [(e * count + t, target(e, t)) for e in range(count) for t in range(count)]
        return lax.ppermute(value, ("expert", "tensor"), pairs)

    def along(value, k):
        return lax.ppermute(value, "expert", [(i, (i + k) % count) for i in range(count)])

    def transposed(value):
        return both(value, lambda e, t: t * count + e)

    with jax.named_scope("gather_cache"):
        cache = prompt_cache.T
        size = key_width // 2
        half = lax.dynamic_slice_in_dim(cache, (tensor & 1) * size, size, 0)
        far_halves = [along(half, k) for k in range(1, count)]
    with jax.named_scope("query_layout"):
        early = (queries, own_latent, cache, value_up)
        q, own, near, vup = pl.pallas_call(
            layout_kernel,
            out_shape=[shape((heads * rows, key_width), BF16)]
            + [pltpu.VMEM(a.shape, a.dtype) for a in early[1:]],
            in_specs=[HBM] * len(early),
            out_specs=[VMEM] * len(early),
            scratch_shapes=[
                pltpu.VMEM(queries.shape, BF16), pltpu.SemaphoreType.DMA((len(early),))
            ],
            compiler_params=pltpu.CompilerParams(vmem_limit_bytes=10 * 1024 * 1024),
            cost_estimate=pl.CostEstimate(
                flops=1000000000, bytes_accessed=30000000, transcendentals=0
            ),
        )(*[pltpu.with_memory_space_constraint(a, pltpu.HBM) for a in early])
    with jax.named_scope("routing"):
        there = transposed(expert_ids.T)
        pick, put, weights, rel = call(
            routing_kernel,
            [
                shape((count, slots, rows), BF16),
                shape((count, rows, slots), BF16),
                shape((rows, count), F32),
                shape((rows, 1), jnp.int32),
            ],
            [SMEM] + [VMEM] * 4,
            (bits, expert_ids.T, there, route_weight.T, row_dest.T),
            0,
        )
    with jax.named_scope("gather_cache"):
        far_halves[0], q = lax.optimization_barrier((far_halves[0], q))
        far_halves[1], pick = lax.optimization_barrier((far_halves[1], pick))
        keys = []
        for part in far_halves:
            keys += [part, swap(part, 1)]
    with jax.named_scope("attend"):
        group = 4
        (far,) = call(
            collect_kernel,
            [shape((count - 1, key_width, prompt), BF16)],
            [SMEM] + [VMEM] * len(keys),
            (bits, *keys),
            0,
        )
        given, far = lax.optimization_barrier((residual_in, far))
        given = transposed(given)
        def attend(start, stop):
            return call(
                functools.partial(attend_kernel, scale, group, start, stop),
                [shape((rows, (stop - start) * vhead), BF16)],
                [VMEM] * 6,
                (rel, q, own, near, far, vup),
                2 * (stop - start) * rows * count * prompt * (key_width + latent),
            )

        (half_out,) = attend(0, heads // 2)
        (half_two,) = attend(heads // 2, heads)
    with jax.named_scope("gather_heads"):
        far_first = across(half_out, 2)
        near_first = across(half_out, 1)
        far_second = across(half_two, 2)
        far_first, near_first, half_two = lax.optimization_barrier(
            (far_first, near_first, half_two)
        )
        near_second = across(half_two, 1)
        last_first = across(far_first, 1)
        last_second = across(far_second, 1)
        given, near_second = lax.optimization_barrier((given, near_second))
    with jax.named_scope("project"):
        (first,) = call(
            project_first_kernel,
            [shape((count * rows, width), F32)],
            [SMEM] + [VMEM] * 5,
            (bits, half_out, near_first, far_first, last_first, out_proj),
            count * rows * heads * vhead * width,
            [pltpu.VMEM((count * rows, heads // 2 * vhead), BF16)],
        )
        kept, sent = call(
            project_kernel,
            [shape((2 * rows, width), F32), shape((2 * rows, width), BF16)],
            [SMEM] + [VMEM] * 6,
            (bits, first, half_two, near_second, far_second, last_second, out_proj),
            count * rows * heads * vhead * width,
            [pltpu.VMEM((count * rows, heads // 2 * vhead), BF16)],
        )
        kept, sent = call(
            halve_kernel,
            [shape((rows, width), F32), shape((rows, width), BF16)],
            [SMEM, VMEM, VMEM],
            (bits, kept, swap(sent, 1)),
            2 * rows * width,
        )
        picked = call(
            resid_kernel,
            [shape((rows, width), BF16)] + [shape((slots, width), BF16)] * (count - 1),
            [VMEM] * 4,
            (kept, swap(sent, 2), given, pick),
            2 * count * rows * slots * width,
        )
    order = (2, 3, 0, 1)
    with jax.named_scope("scatter_resid"):
        arrived = [
            both(picked[k], lambda e, t, k=k: (t + k) % count * count + e) for k in order
        ]
        resid = arrived[order.index(0)]
    wide = 2 * ff + 128
    with jax.named_scope("expand"):
        kept, sent = call(
            expand_kernel,
            [shape((2 * slots, wide), BF16), shape((2 * slots, wide), BF16)],
            [SMEM] + [VMEM] * 8,
            (bits, pick, *arrived, norm_gain[None, :], gate_weight[0], up_weight[0]),
            4 * count * slots * width * ff,
        )
        halves = call(
            add_expand_kernel,
            [shape((slots, wide), F32), shape((slots, wide), BF16)] * 2,
            [VMEM, VMEM],
            (kept, swap(sent, 1)),
            2 * slots * wide,
        )
    outs = []
    for n in range(2):
        kept, sent = halves[2 * n : 2 * n + 2]
        with jax.named_scope("expand"):
            got = swap(sent, 2)
            if n == 1:
                *outs, got = lax.optimization_barrier((*outs, got))
            (hidden,) = call(
                functools.partial(hidden_kernel, width * count),
                [shape((slots, ff), BF16)],
                [VMEM, VMEM],
                (kept, got),
                8 * slots * wide,
            )
        with jax.named_scope("contract"):
            outs += call(
                contract_kernel,
                [shape((slots, width), BF16)] * 2,
                [SMEM] + [VMEM] * 3,
                (bits, hidden, swap(hidden, 1), down_weight[0]),
                4 * slots * width * ff,
                [pltpu.VMEM((2 * slots, ff), BF16)],
            )
    with jax.named_scope("combine"):
        back = [along(out, -k) if k else out for k, out in sorted(zip(order, outs), key=lambda pair: pair[0])]
        (early,) = call(
            combine_early_kernel,
            [shape((rows, width), F32)],
            [VMEM] * 6,
            (put, weights, resid, back[0], back[2], back[3]),
            6 * rows * slots * width,
        )
        (scored,) = call(
            combine_kernel,
            [shape((rows, width), BF16)],
            [VMEM] * 4,
            (put, weights, early, back[1]),
            2 * rows * slots * width,
        )
    return scored


def slot_table(targets, count, capacity):
    onehot = (targets[:, None] == jnp.arange(count, dtype=jnp.int32)[None, :]).astype(jnp.int32)
    before = jnp.cumsum(onehot, axis=0) - onehot
    rank = jnp.sum(before * onehot, axis=1)
    return targets * capacity + rank


def general(
    queries,
    own_latent,
    residual_in,
    row_dest,
    prompt_cache,
    value_up,
    out_proj,
    norm_gain,
    gate_weight,
    up_weight,
    down_weight,
    expert_ids,
    route_weight,
):
    shards = lax.axis_size("expert")
    tok_rows = residual_in.shape[0]
    width_part = residual_in.shape[1]
    heads_here = value_up.shape[0]
    latent = value_up.shape[1]
    vhead = value_up.shape[2]
    key_width = own_latent.shape[1]
    scale = (vhead + key_width - latent) ** (-0.5)
    capacity = max(2, 2 * tok_rows // shards)
    total_slots = shards * capacity
    slot = slot_table(row_dest[:, 0], shards, capacity)
    send_query = jnp.zeros((total_slots, queries.shape[1]), queries.dtype).at[slot].set(queries)
    send_key = jnp.zeros((total_slots, key_width), own_latent.dtype).at[slot].set(own_latent)
    recv_query, recv_key = (
        lax.all_to_all(send_query, "expert", split_axis=0, concat_axis=0, tiled=True),
        lax.all_to_all(send_key, "expert", split_axis=0, concat_axis=0, tiled=True),
    )
    query_heads = recv_query.reshape(total_slots, heads_here, key_width)
    scores = (
        jnp.einsum("shc,pc->shp", query_heads, prompt_cache, preferred_element_type=jnp.float32)
        * scale
    )
    own_score = (
        jnp.einsum("shc,sc->sh", query_heads, recv_key, preferred_element_type=jnp.float32) * scale
    )
    top = jnp.maximum(jnp.max(scores, axis=2), own_score)
    expo = jnp.exp(scores - top[:, :, None])
    own_e = jnp.exp(own_score - top)
    total = jnp.sum(expo, axis=2) + own_e
    probs = (expo / total[:, :, None]).astype(jnp.bfloat16)
    own_p = (own_e / total).astype(jnp.bfloat16)
    latent_out = jnp.einsum(
        "shp,pl->shl", probs, prompt_cache[:, :latent], preferred_element_type=jnp.float32
    )
    latent_out = latent_out + own_p.astype(jnp.float32)[:, :, None] * recv_key[
        :, None, :latent
    ].astype(jnp.float32)
    latent_out = latent_out.astype(jnp.bfloat16)
    head_out = jnp.einsum(
        "shl,hlv->shv", latent_out, value_up, preferred_element_type=jnp.float32
    ).astype(jnp.bfloat16)
    head_out = head_out.reshape(total_slots, heads_here * vhead)
    returned_heads = lax.all_to_all(head_out, "expert", split_axis=0, concat_axis=0, tiled=True)
    attn_rows = returned_heads[slot]
    partial_value = jnp.dot(
        attn_rows,
        lax.all_gather(out_proj, "expert", axis=1, tiled=True),
        preferred_element_type=jnp.float32,
    )
    attn_part = lax.psum_scatter(
        partial_value.astype(jnp.bfloat16), "tensor", scatter_dimension=1, tiled=True
    ).astype(jnp.float32)
    resid = residual_in.astype(jnp.float32) + attn_part
    squares = lax.psum(jnp.sum(resid * resid, axis=1), "tensor")
    full_width = width_part * lax.axis_size("tensor")
    normed = (
        resid * lax.rsqrt(squares / full_width + 1e-06)[:, None] * norm_gain.astype(jnp.float32)
    ).astype(jnp.bfloat16)
    topk = expert_ids.shape[1]
    cap_x = 3 * topk * tok_rows // (2 * shards)
    assign_slot = slot_table(expert_ids.reshape(-1), shards, cap_x)
    assign_row = jnp.arange(tok_rows * topk, dtype=jnp.int32) // topk
    send_rows = (
        jnp.zeros((shards * cap_x, width_part), jnp.bfloat16)
        .at[assign_slot]
        .set(normed[assign_row])
    )
    arrived = lax.all_to_all(send_rows, "expert", split_axis=0, concat_axis=0, tiled=True)
    gate_part = (
        jnp.dot(arrived, gate_weight[0], preferred_element_type=jnp.float32)
        .astype(jnp.bfloat16)
        .astype(jnp.float32)
    )
    up_part = (
        jnp.dot(arrived, up_weight[0], preferred_element_type=jnp.float32)
        .astype(jnp.bfloat16)
        .astype(jnp.float32)
    )
    gate_sum, up_sum = (
        lax.psum(gate_part.astype(jnp.bfloat16), "tensor").astype(jnp.float32),
        lax.psum(up_part.astype(jnp.bfloat16), "tensor").astype(jnp.float32),
    )
    hidden = (jax.nn.silu(gate_sum) * up_sum).astype(jnp.bfloat16)
    expert_out = jnp.dot(hidden, down_weight[0], preferred_element_type=jnp.float32).astype(
        jnp.bfloat16
    )
    came_back = lax.all_to_all(expert_out, "expert", split_axis=0, concat_axis=0, tiled=True)
    picked = came_back[assign_slot].astype(jnp.float32).reshape(tok_rows, topk, width_part)
    moe = jnp.sum(route_weight[:, :, None] * picked, axis=1)
    return (resid + moe).astype(jnp.bfloat16)


def local(*args):
    if lax.axis_size("expert") == 4 and lax.axis_size("tensor") == 4:
        return square(*args)
    return general(*args)


def solution(mesh):
    return jax.shard_map(
        local,
        mesh=mesh,
        in_specs=(
            P(("groups", "expert"), "tensor"),
            P(("groups", "expert"), None),
            P(("groups", "expert"), "tensor"),
            P(("groups", "expert"), None),
            P(("groups", "expert"), None),
            P("tensor", None, None),
            P("tensor", "expert"),
            P("tensor"),
            P("expert", "tensor", None),
            P("expert", "tensor", None),
            P("expert", None, "tensor"),
            P(("groups", "expert"), None),
            P(("groups", "expert"), None),
        ),
        out_specs=P(("groups", "expert"), "tensor"),
        check_vma=False,
    )
```
